256 devices in a mesh: pts: 64 (over x, z, core), head: 4 (over y).
Axes of the slice: x: 4, y: 4, z: 8, core: 2. Of those that a mesh axis runs over, the one named last changes fastest.
Arguments:
- feats: bfloat16 [65536, 512], P('pts'), may hold values from -6 to 6
- neighbours: int32 [65536, 27], P('pts'), may hold values from -1 to 65535, as said below
- rank: int32 [65536], P('pts'), may hold values from 0 to 65535, as said below
- conv_weight: bfloat16 [27, 512, 512], P(None, None, 'head'), may hold values from -0.0546875 to 0.0546875
- cpe_gain: float32 [512], replicated, may hold values from 0.1 to 1.9
- norm1_gain: float32 [512], replicated, may hold values from 0.1 to 1.9
- w_query: bfloat16 [512, 512], P(None, 'head'), may hold values from -0.27 to 0.27
- w_key: bfloat16 [512, 512], P(None, 'head'), may hold values from -9 to 9
- w_value: bfloat16 [512, 512], P(None, 'head'), may hold values from -0.25 to 0.25
- w_proj: bfloat16 [512, 512], replicated, may hold values from -0.25 to 0.25
- norm2_gain: float32 [512], replicated, may hold values from 0.1 to 1.9
- w_fc1: bfloat16 [512, 2048], replicated, may hold values from -0.25 to 0.25
- w_fc2: bfloat16 [2048, 512], replicated, may hold values from -0.125 to 0.125
Outputs:
- block_out: bfloat16 [65536, 512], P('pts')
The draws below stay inside these ranges and needn't reach their ends.
Inputs may be any that keep to these rules, and one draw needn't show every extreme that they name: `rank`: A permutation of the points. The points that one device holds (rows of 1024) reach the position range of any one device ([d * 1024, (d + 1) * 1024)) at most 28 times, and exactly 28 times for some pairs of devices in every draw. `neighbours`: tap (27 - 1) // 2 is the point itself; any other entry is -1 or an index j with 0 < |j - i| <= 256 (taps below the middle point backwards, the others forwards); the distance 256 is reached in every draw.
All inputs are finite; a program needn't handle non-finite values.
Results may differ from the reference program's by a relative error of at most 0.013.
The reference program's roundings to bfloat16 on the way (of `conv`, `normed`, `probs`, `attended`, `merged`, `normed2` and `hidden`) count: a program that leaves them out, or rounds other values in their place, can miss the bound.
Values may be sent and summed in bfloat16 or wider, within the bound.
A program may use at most 192 MiB of HBM per device.

```python
import jax
import jax.numpy as jnp
from jax import lax

C = 512
HEADS = 32
HD = 16
MLP_UNITS = 2048
PATCH = 1024
TAPS = 27
PTS_DEV = 1024
POINTS = 65536


def shared_query(key):
    base = jnp.clip(jax.random.normal(jax.random.fold_in(key, 11), (C, C), jnp.float32), -6.0, 6.0) * C ** (-0.5)
    return jnp.clip(base, -0.27, 0.27)


def draw_w_query(key, part):
    base = shared_query(key)
    return base.astype(jnp.bfloat16)


def draw_w_key(key, part):
    key = jax.random.fold_in(key, 17)
    own = jnp.clip(jax.random.normal(key, (C, C), jnp.float32), -6.0, 6.0) * C ** (-0.5)
    return own.astype(jnp.bfloat16)


def draw_rank(key, part):
    key = jax.random.fold_in(key, 5)
    devices = POINTS // PTS_DEV
    share = PTS_DEV // (4 * devices)
    key_off, key_src, key_dst = jax.random.split(key, 3)
    offsets = jax.random.permutation(key_off, devices).astype(jnp.int32)
    levels = jnp.array([7, 1, 5, 3], jnp.int32)
    weights = levels[jnp.arange(devices) % 4] * share
    ends = jnp.cumsum(weights)
    which = jnp.searchsorted(ends, jnp.arange(PTS_DEV, dtype=jnp.int32), side='right').astype(jnp.int32)
    sigma = jax.vmap(lambda k: jax.random.permutation(k, PTS_DEV))(jax.random.split(key_src, devices)).astype(jnp.int32)
    tau = jax.vmap(lambda k: jax.random.permutation(k, PTS_DEV))(jax.random.split(key_dst, devices)).astype(jnp.int32)
    source = jnp.arange(devices, dtype=jnp.int32)[:, None]
    target = (source + offsets[which[sigma]]) % devices
    position = tau[target, sigma]
    return (target * PTS_DEV + position).reshape(-1).astype(jnp.int32)


def draw_neighbours(key, part):
    key = jax.random.fold_in(key, 7)
    key_step, key_gone = jax.random.split(key)
    reach = PTS_DEV // 4
    middle = (TAPS - 1) // 2
    tap = jnp.arange(TAPS, dtype=jnp.int32)[None, :]
    point = jnp.arange(POINTS, dtype=jnp.int32)[:, None]
    steps = jax.random.randint(key_step, (POINTS, TAPS), 1, reach + 1).astype(jnp.int32)
    forced = (point % 97 == 0) & ((tap == 0) | (tap == TAPS - 1))
    steps = jnp.where(forced, reach, steps)
    signs = jnp.where(tap < middle, -1, 1)
    target = jnp.where(tap == middle, point, point + signs * steps)
    absent = (jax.random.randint(key_gone, (POINTS, TAPS), 0, 3) == 0) & (tap != middle) & jnp.logical_not(forced)
    target = jnp.where(absent | (target < 0) | (target >= POINTS), -1, target)
    return target.astype(jnp.int32)


def shard_levels(rng, shape, cuts, low, largest):
    factor_of = 1.0
    for axis_at, parts in cuts:
        draws = jax.random.uniform(jax.random.fold_in(jax.random.fold_in(rng, 6), axis_at), (parts,), jnp.float32, low / len(cuts), largest / len(cuts))
        factor_of = factor_of * jnp.repeat(jnp.exp(draws), shape[axis_at] // parts).reshape((-1,) + (1,) * (len(shape) - 1 - axis_at))
    return factor_of


def centred(key, shape, deviation, most, cuts=(), held_as=jnp.bfloat16):
    values = jax.random.normal(key, shape, jnp.float32) * deviation
    if len(cuts) > 0:
        values = shard_levels(key, shape, cuts, -0.22, 0.18) * values
    return jnp.clip(values, min=-most, max=most).astype(held_as)


def setup_inputs(seed: int = 0) -> dict:
    key_list = jax.random.split(jax.random.key(seed), 14)
    feats = centred(key_list[0], (POINTS, C), 1.0, 6.0, ((0, 64),))
    neighbours = draw_neighbours(jax.random.fold_in(key_list[13], 71), 0)
    rank = draw_rank(jax.random.fold_in(key_list[13], 71), 0)
    conv_weight = centred(key_list[3], (TAPS, C, C), (TAPS * C) ** -0.5, 0.0546875, ((2, 4),))
    cpe_gain = jnp.clip(1.0 + 0.18 * jax.random.normal(key_list[4], (C,), jnp.float32), 0.1, 1.9)
    norm1_gain = jnp.clip(1.0 + 0.18 * jax.random.normal(key_list[5], (C,), jnp.float32), 0.1, 1.9)
    w_query = draw_w_query(jax.random.fold_in(key_list[13], 71), 0)
    w_key = draw_w_key(jax.random.fold_in(key_list[13], 71), 0)
    w_value = centred(key_list[8], (C, C), C ** -0.5, 0.25, ((1, 4),))
    w_proj = centred(key_list[9], (C, C), C ** -0.5, 0.25)
    norm2_gain = jnp.clip(1.0 + 0.18 * jax.random.normal(key_list[10], (C,), jnp.float32), 0.1, 1.9)
    w_fc1 = centred(key_list[11], (C, MLP_UNITS), C ** -0.5, 0.25)
    w_fc2 = centred(key_list[12], (MLP_UNITS, C), MLP_UNITS ** -0.5, 0.125)
    return dict(feats=feats, neighbours=neighbours, rank=rank, conv_weight=conv_weight, cpe_gain=cpe_gain, norm1_gain=norm1_gain, w_query=w_query, w_key=w_key, w_value=w_value, w_proj=w_proj, norm2_gain=norm2_gain, w_fc1=w_fc1, w_fc2=w_fc2)


def layer_norm(values, gain):
    centre = values - lax.optimization_barrier(jnp.mean(values, -1, keepdims=True))
    spread = lax.optimization_barrier(jnp.mean(centre * centre, -1, keepdims=True))
    return centre * lax.rsqrt(spread + 1e-05) * gain

def patch_attention(queries, keys_all, values_all):
    scores = jnp.einsum('qhd,khd->hqk', queries.astype(jnp.float32), keys_all.astype(jnp.float32)) / jnp.sqrt(jnp.float32(HD))
    probs = jax.nn.softmax(scores, axis=-1).astype(jnp.bfloat16)
    attended = jnp.einsum('hqk,khd->qhd', probs.astype(jnp.float32), values_all.astype(jnp.float32))
    return attended.astype(jnp.bfloat16)

def reference(feats, neighbours, rank, conv_weight, cpe_gain, norm1_gain, w_query, w_key, w_value, w_proj, norm2_gain, w_fc1, w_fc2):
    padded = jnp.concatenate([feats, jnp.zeros((1, C), jnp.bfloat16)], 0)
    chosen = jnp.where(neighbours < 0, POINTS, neighbours).astype(jnp.int32)
    conv = jnp.zeros((POINTS, C), jnp.float32)
    for tap in range(TAPS):
        conv = conv + jnp.dot(padded[chosen[:, tap]], conv_weight[tap], preferred_element_type=jnp.float32)
    conv = conv.astype(jnp.bfloat16)
    h_one = feats.astype(jnp.float32) + layer_norm(conv.astype(jnp.float32), cpe_gain)
    normed = layer_norm(h_one, norm1_gain).astype(jnp.bfloat16)
    queries = jnp.dot(normed, w_query, preferred_element_type=jnp.float32).astype(jnp.bfloat16)
    keys_all = jnp.dot(normed, w_key, preferred_element_type=jnp.float32).astype(jnp.bfloat16)
    values_all = jnp.dot(normed, w_value, preferred_element_type=jnp.float32).astype(jnp.bfloat16)
    order = jnp.zeros((POINTS,), jnp.int32).at[rank].set(jnp.arange(POINTS, dtype=jnp.int32))
    patches = POINTS // PATCH
    shaped = [a[order].reshape(patches, PATCH, HEADS, HD) for a in (queries, keys_all, values_all)]
    attended = lax.map(lambda group: patch_attention(*group), tuple(shaped))
    attended = attended.reshape(POINTS, C)[rank]
    merged = jnp.dot(attended, w_proj, preferred_element_type=jnp.float32).astype(jnp.bfloat16)
    h_two = h_one + merged.astype(jnp.float32)
    normed2 = layer_norm(h_two, norm2_gain).astype(jnp.bfloat16)
    hidden = jax.nn.gelu(jnp.dot(normed2, w_fc1, preferred_element_type=jnp.float32), approximate=False).astype(jnp.bfloat16)
    return (h_two + jnp.dot(hidden, w_fc2, preferred_element_type=jnp.float32)).astype(jnp.bfloat16)
```

```python
import functools

import jax
import jax.numpy as jnp
import numpy as np
from jax import lax
from jax.experimental import pallas as pl
from jax.experimental.pallas import tpu as pltpu
from jax.sharding import PartitionSpec as P

HD = 16
PTS = 1024
REACH = 256
TAPS = 27
MID = 13
C = 512
W = 128
DEVS = 64
SLOTS = 32
ROWS = DEVS * SLOTS
BLK = 256
BF = jnp.bfloat16
F32 = jnp.float32
I32 = jnp.int32
VMEM = pltpu.MemorySpace.VMEM


def iota(shape, dim):
    return lax.broadcasted_iota(I32, shape, dim)


def dot(a, b):
    return jnp.dot(a, b, preferred_element_type=F32)


def dot_nt(a, b):
    return lax.dot_general(a, b, (((1,), (1,)), ((), ())), preferred_element_type=F32)


def hot(mask):
    return jnp.where(mask, 1.0, 0.0).astype(BF)


def conv_project(ext_ref, w_ref, yb_ref, yf_ref):
    for start, first, count, y_ref in ((0, 0, MID + 1, yb_ref), (REACH, MID + 1, MID, yf_ref)):
        rows = ext_ref.at[pl.ds(start, PTS + REACH)]

        @pl.loop(0, count // 2)
        def _(j):
            pair = jnp.concatenate([w_ref[first + 2 * j], w_ref[first + 2 * j + 1]], 1)
            y = dot(rows[...], pair).astype(BF)
            y_ref[2 * j] = y[:, :W]
            y_ref[2 * j + 1] = y[:, W:]

        if count % 2:
            y_ref[count - 1] = dot(rows[...], w_ref[first + count - 1]).astype(BF)


def conv_select(a, base, nbr_ref, yb_ref, yf_ref):
    start = pl.multiple_of(a * BLK, BLK)
    nbr = nbr_ref[pl.ds(start, BLK), :]
    at = nbr - (base + start)
    at = jnp.where(nbr < 0, -4096, at)
    window = iota((BLK, 2 * BLK), 1)
    acc = yb_ref[MID, pl.ds(start + REACH, BLK), :].astype(F32)
    for t in range(TAPS):
        if t == MID:
            continue
        if t < MID:
            sel = hot(window == at[:, t : t + 1] + REACH)
            acc += dot(sel, yb_ref[t, pl.ds(start, 2 * BLK), :])
        else:
            sel = hot(window == at[:, t : t + 1])
            acc += dot(sel, yf_ref[t - MID - 1, pl.ds(start, 2 * BLK), :])
    return acc


def conv_kernel(base_ref, ext_ref, nbr_ref, w_ref, out_ref, yb_ref, yf_ref):
    conv_project(ext_ref, w_ref, yb_ref, yf_ref)

    @pl.loop(0, PTS // BLK)
    def _(a):
        acc = conv_select(a, base_ref[0], nbr_ref, yb_ref, yf_ref)
        out_ref[pl.ds(pl.multiple_of(a * BLK, BLK), BLK), :] = acc.astype(BF)


def norm_slices(parts, gain_ref):
    mean = sum(jnp.sum(p, 1, keepdims=True) for p in parts) * (1.0 / C)
    centre = [p - mean for p in parts]
    spread = sum(jnp.sum(c * c, 1, keepdims=True) for c in centre) * (1.0 / C)
    scale = lax.rsqrt(spread + 1e-05)
    return [c * scale * gain_ref[:, W * k : W * k + W] for k, c in enumerate(centre)]


def mid_block(a, conv_ref, feats_ref, cpe_ref, n1_ref, h1_ref, normed_ref):
    rows = pl.ds(pl.multiple_of(a * BLK, BLK), BLK)
    conv = [conv_ref[k, rows, :].astype(F32) for k in range(4)]
    normed = norm_slices(conv, cpe_ref)
    h1 = [feats_ref[rows, W * k : W * k + W].astype(F32) + normed[k] for k in range(4)]
    for k, part in enumerate(norm_slices(h1, n1_ref)):
        h1_ref[rows, W * k : W * k + W] = h1[k]
        normed_ref[k, rows, :] = part.astype(BF)


def bucket_of_row(rank_row):
    target = rank_row // PTS
    ohT = hot(iota((DEVS, PTS), 0) == target)
    upper = hot(iota((PTS, PTS), 0) < iota((PTS, PTS), 1))
    counts = dot(ohT, upper)
    slot = jnp.sum(counts * ohT.astype(F32), 0, keepdims=True).astype(I32)
    code = rank_row % PTS + 1
    by_slot = hot(iota((W, PTS), 0) == slot)
    ohf = ohT.astype(F32)
    high = dot_nt((ohf * (code // 32).astype(F32)).astype(BF), by_slot)
    low = dot_nt((ohf * (code % 32).astype(F32)).astype(BF), by_slot)
    return target * SLOTS + slot, jnp.concatenate([high, low], 0).astype(BF)


def bucket_of_column(rank_col):
    target = rank_col // PTS
    oh = hot(iota((PTS, DEVS), 1) == target)
    lower = hot(iota((PTS, PTS), 1) < iota((PTS, PTS), 0))
    counts = dot(lower, oh)
    slot = jnp.sum(counts * oh.astype(F32), 1, keepdims=True).astype(I32)
    return target * SLOTS + slot


def pack_rows(bucket_row, positions, own, out_ref):
    @pl.loop(0, ROWS // BLK)
    def _(b):
        start = pl.multiple_of(b * BLK, BLK)
        sel = hot(iota((BLK, PTS), 0) + start == bucket_row)
        r = iota((BLK, W), 0) + start
        c = iota((BLK, W), 1)
        s = r % SLOTS
        d = r // SLOTS
        place = hot(((s == 28) & (c == d)) | ((s == 29) & (c == d + DEVS)))
        out_ref[pl.ds(start, BLK), :] = (dot(sel, own) + dot(place, positions)).astype(BF)


def digits_of(arrived):
    r = iota((DEVS, ROWS), 1)
    q = iota((DEVS, ROWS), 0)
    high = dot(hot(r == q * SLOTS + 28), arrived).astype(BF)
    low = dot(hot(r == q * SLOTS + 29), arrived).astype(BF)
    return high, low


def spots_row(high, low):
    pick = hot(iota((W, ROWS), 0) == iota((W, ROWS), 1) % SLOTS)
    full = dot(high, pick) * 32.0 + dot(low, pick) - 1.0
    mine = iota((DEVS, ROWS), 0) == iota((DEVS, ROWS), 1) // SLOTS
    return jnp.sum(jnp.where(mine, full, 0.0), 0, keepdims=True).astype(I32)


def spots_column(high, low, start, count):
    r = iota((count, DEVS), 0) + start
    pick = hot(iota((count, DEVS), 1) == r // SLOTS)
    full = dot(pick, high) * 32.0 + dot(pick, low) - 1.0
    mine = iota((count, W), 1) == (iota((count, W), 0) + start) % SLOTS
    return jnp.sum(jnp.where(mine, full, 0.0), 1, keepdims=True).astype(I32)


def place_rows(spots, arrived_ref, out_ref):
    @pl.loop(0, PTS // BLK)
    def _(b):
        start = pl.multiple_of(b * BLK, BLK)
        sel = hot(iota((BLK, ROWS), 0) + start == spots)
        out_ref[pl.ds(start, BLK), :] = dot(sel, arrived_ref[...]).astype(BF)


def unplace_rows(high, low, own_ref, out_ref):
    @pl.loop(0, ROWS // BLK)
    def _(b):
        start = pl.multiple_of(b * BLK, BLK)
        spots = spots_column(high, low, start, BLK)
        sel = hot(iota((BLK, PTS), 1) == spots)
        out_ref[pl.ds(start, BLK), :] = dot(sel, own_ref[...]).astype(BF)


def unpack_rows(bucket_col_ref, returned_ref, out_ref):
    @pl.loop(0, PTS // BLK)
    def _(b):
        start = pl.multiple_of(b * BLK, BLK)
        bucket = bucket_col_ref[pl.ds(start, BLK), :]
        sel = hot(iota((BLK, ROWS), 1) == bucket)
        out_ref[pl.ds(start, BLK), :] = dot(sel, returned_ref[...]).astype(BF)


def mid_kernel(conv_ref, feats_ref, rank_ref, cpe_ref, n1_ref, h1_ref, out_ref, normed_ref):
    @pl.loop(0, PTS // BLK)
    def _(a):
        mid_block(a, conv_ref, feats_ref, cpe_ref, n1_ref, h1_ref, normed_ref)

    bucket, positions = bucket_of_row(rank_ref[...])
    pack_rows(bucket, positions, normed_ref[lax.axis_index("head")], out_ref)


def place_kernel(arrived_ref, out_ref):
    high, low = digits_of(arrived_ref[...])
    place_rows(spots_row(high, low), arrived_ref, out_ref)


def attend(x_ref, wq_ref, wk_ref, wv_ref, qq_ref, k_ref, v_ref, acc_ref, att_ref):
    def project(w_ref):
        return sum(dot(x_ref[k], w_ref[W * k : W * k + W, :]) for k in range(4)).astype(BF)

    scaled = project(wq_ref).astype(F32) * np.float32(np.log2(np.e) / 4.0)
    high = scaled.astype(BF)
    qq_ref[:, :W] = high
    qq_ref[:, W:] = (scaled - high.astype(F32)).astype(BF)
    k_ref[...] = project(wk_ref)
    v_ref[...] = project(wv_ref)
    acc_ref[...] = jnp.zeros_like(acc_ref)
    lane = iota((PTS, W), 1) // HD

    @pl.loop(0, W // HD)
    def _(h):
        own = lane == h
        zero = jnp.zeros((PTS, W), BF)
        keys = jnp.where(own, k_ref[...], zero)
        keys = jnp.concatenate([keys, keys], 1)
        values = jnp.concatenate([jnp.where(own, v_ref[...], zero), hot(own)], 1)
        for b in range(PTS // BLK):
            rows = slice(b * BLK, b * BLK + BLK)
            scores = dot_nt(qq_ref[rows, :], keys)
            top = jnp.max(scores, 1, keepdims=True)
            probs = jnp.exp2(scores - top).astype(BF)
            acc_ref[rows, :] += dot(probs, values)

    att_ref[...] = (acc_ref[:, :W] / acc_ref[:, W:]).astype(BF)


def attend_kernel(
    x_ref, arrived_ref, wq_ref, wk_ref, wv_ref, out_ref, qq_ref, k_ref, v_ref, acc_ref, att_ref
):
    attend(x_ref, wq_ref, wk_ref, wv_ref, qq_ref, k_ref, v_ref, acc_ref, att_ref)
    high, low = digits_of(arrived_ref[...])
    unplace_rows(high, low, att_ref, out_ref)


def unpack_kernel(returned_ref, rank_ref, out_ref, bucket_ref):
    bucket_ref[...] = bucket_of_column(rank_ref[...])
    unpack_rows(bucket_ref, returned_ref, out_ref)


def mlp_block(a, att_ref, h1_ref, wp_ref, n2_ref, f1_ref, f2_ref, out_ref):
    rows = pl.ds(pl.multiple_of(a * BLK, BLK), BLK)
    merged = sum(dot(att_ref[k, rows, :], wp_ref[W * k : W * k + W, :]) for k in range(4))
    h2 = h1_ref[rows, :] + merged.astype(BF).astype(F32)
    parts = norm_slices([h2[:, W * k : W * k + W] for k in range(4)], n2_ref)
    normed = jnp.concatenate([p.astype(BF) for p in parts], 1)
    total = h2
    for j in range(4):
        cols = slice(C * j, C * j + C)
        x = dot(normed, f1_ref[:, cols])
        hidden = (0.5 * x * (1.0 + lax.erf(x * np.float32(np.sqrt(0.5))))).astype(BF)
        total += dot(hidden, f2_ref[cols, :])
    out_ref[rows, :] = total.astype(BF)


def mlp_kernel(att_ref, h1_ref, wp_ref, n2_ref, f1_ref, f2_ref, out_ref):
    @pl.loop(0, PTS // BLK)
    def _(a):
        mlp_block(a, att_ref, h1_ref, wp_ref, n2_ref, f1_ref, f2_ref, out_ref)


def call(kernel, outs, scratch, *args, smem=0):
    spaces = [pltpu.MemorySpace.SMEM] * smem + [VMEM] * (len(args) - smem)
    many = isinstance(outs, (list, tuple))
    return pl.pallas_call(
        kernel,
        out_shape=outs,
        in_specs=[pl.BlockSpec(memory_space=s) for s in spaces],
        out_specs=[pl.BlockSpec(memory_space=VMEM)] * len(outs)
        if many
        else pl.BlockSpec(memory_space=VMEM),
        scratch_shapes=scratch,
        compiler_params=pltpu.CompilerParams(vmem_limit_bytes=48 * 2**20),
    )(*args)


def shape(dims, dtype=BF):
    return jax.ShapeDtypeStruct(dims, dtype)


def conv_local(base, ext, neighbours, conv_weight):
    return call(
        conv_kernel,
        shape((PTS, W)),
        [pltpu.VMEM((MID + 1, PTS + REACH, W), BF), pltpu.VMEM((MID, PTS + REACH, W), BF)],
        base,
        ext,
        neighbours,
        conv_weight,
        smem=1,
    )


def attend_local(x, arrived, w_query, w_key, w_value):
    return call(
        attend_kernel,
        shape((ROWS, W)),
        [
            pltpu.VMEM((PTS, 2 * W), BF),
            pltpu.VMEM((PTS, W), BF),
            pltpu.VMEM((PTS, W), BF),
            pltpu.VMEM((PTS, 2 * W), F32),
            pltpu.VMEM((PTS, W), BF),
        ],
        x,
        arrived,
        w_query,
        w_key,
        w_value,
    )


def exchange(rows):
    blocks = rows.reshape(DEVS, SLOTS, W)
    return lax.all_to_all(blocks, "pts", split_axis=0, concat_axis=0, tiled=True).reshape(ROWS, W)


def per_device(
    feats,
    neighbours,
    rank,
    conv_weight,
    cpe_gain,
    norm1_gain,
    w_query,
    w_key,
    w_value,
    w_proj,
    norm2_gain,
    w_fc1,
    w_fc2,
):
    count = lax.axis_size("pts")
    me = lax.axis_index("pts")
    up = [(i, i + 1) for i in range(count - 1)]
    down = [(i + 1, i) for i in range(count - 1)]
    ext = jnp.concatenate(
        [
            lax.ppermute(feats[PTS - REACH :], "pts", up),
            feats,
            lax.ppermute(feats[:REACH], "pts", down),
        ],
        0,
    )
    base = (me * PTS).astype(I32).reshape(1)
    conv = conv_local(base, ext, neighbours, conv_weight)
    conv_full = lax.all_gather(conv, "head", axis=0, tiled=False)
    rank_row, rank_col = rank.reshape(1, PTS), rank.reshape(PTS, 1)
    h_one, outgoing = call(
        mid_kernel,
        [shape((PTS, C), F32), shape((ROWS, W))],
        [pltpu.VMEM((4, PTS, W), BF)],
        conv_full,
        feats,
        rank_row,
        cpe_gain.reshape(1, C),
        norm1_gain.reshape(1, C),
    )
    arrived = exchange(outgoing)
    placed = call(place_kernel, shape((PTS, W)), [], arrived)
    placed_full = lax.all_gather(placed, "head", axis=0, tiled=False)
    rows_back = attend_local(placed_full, arrived, w_query, w_key, w_value)
    returned = exchange(rows_back)
    attended = call(
        unpack_kernel, shape((PTS, W)), [pltpu.VMEM((PTS, 1), I32)], returned, rank_col
    )
    attended_full = lax.all_gather(attended, "head", axis=0, tiled=False)
    return call(
        mlp_kernel,
        shape((PTS, C)),
        [],
        attended_full,
        h_one,
        w_proj,
        norm2_gain.reshape(1, C),
        w_fc1,
        w_fc2,
    )


def solution(mesh):
    placed = (
        P("pts", None),
        P("pts", None),
        P("pts"),
        P(None, None, "head"),
        P(),
        P(),
        P(None, "head"),
        P(None, "head"),
        P(None, "head"),
        P(),
        P(),
        P(),
        P(),
    )
    return jax.shard_map(
        per_device, mesh=mesh, in_specs=placed, out_specs=P("pts", None), check_vma=False
    )
```

```python
import jax
import jax.numpy as jnp
import numpy as np
from jax import lax
from jax.experimental import pallas as pl
from jax.experimental.pallas import tpu as pltpu
from jax.sharding import PartitionSpec as P

HD = 16
PTS = 1024
REACH = 256
TAPS = 27
MID = 13
C = 512
MLP = 2048
W = 128
HEADS = 4
DEVS = 64
SLOTS = 32
ROWS = DEVS * SLOTS
NOTE = 16
BLK = 256
CHUNKS = PTS // BLK
GROUP = BLK // SLOTS
BF = jnp.bfloat16
F32 = jnp.float32
I32 = jnp.int32
VMEM = pltpu.MemorySpace.VMEM
MESH = pl.DeviceIdType.MESH


def iota(shape, dim):
    return lax.broadcasted_iota(I32, shape, dim)


def dot(a, b):
    return jnp.dot(a, b, preferred_element_type=F32)


def dot_nt(a, b):
    return lax.dot_general(a, b, (((1,), (1,)), ((), ())), preferred_element_type=F32)


def hot(mask):
    return jnp.where(mask, 1.0, 0.0).astype(BF)


def block(a, size=BLK):
    return pl.ds(pl.multiple_of(a * size, size), size)


def barrier_signal(p, h):
    barrier = pltpu.get_barrier_semaphore()

    @pl.loop(1, DEVS)
    def _(k):
        pl.semaphore_signal(
            barrier, inc=1, device_id=(lax.rem(p + k, DEVS), h), device_id_type=MESH
        )

    for k in (1, HEADS - 1):
        pl.semaphore_signal(
            barrier, inc=1, device_id=(p, lax.rem(h + k, HEADS)), device_id_type=MESH
        )


def barrier_wait():
    pl.semaphore_wait(pltpu.get_barrier_semaphore(), DEVS + 1)


def send_block(p, h, d, size, out_ref, in_ref, send_sem, recv_sem):
    pltpu.make_async_remote_copy(
        src_ref=out_ref.at[block(d, size)],
        dst_ref=in_ref.at[block(p, size)],
        send_sem=send_sem,
        recv_sem=recv_sem,
        device_id=(d, h),
        device_id_type=MESH,
    ).start()


def wait_blocks(size, ref, sem):
    part = ref.at[pl.ds(0, (DEVS - 1) * size)]
    pltpu.make_async_copy(part, part, sem).wait()


class Gather:
    def __init__(self, p, h, ref, send_sem, recv_sem):
        self.p, self.h, self.ref, self.send_sem, self.recv_sem = p, h, ref, send_sem, recv_sem
        self.right, self.left = lax.rem(h + 1, HEADS), lax.rem(h + 3, HEADS)
        self.far = lax.rem(h + 2, HEADS)

    def copy(self, kind, c):
        owner, upper, to = (
            (self.h, True, self.right),
            (self.h, False, self.left),
            (self.h, False, self.right),
            (self.h, True, self.left),
            (self.left, True, self.right),
            (self.right, False, self.left),
        )[kind]
        half = BLK // 2
        start = pl.multiple_of(c * BLK + (0 if upper else half), half)
        rows = self.ref.at[owner, pl.ds(start, half)]
        return pltpu.make_async_remote_copy(
            src_ref=rows,
            dst_ref=rows,
            send_sem=self.send_sem.at[kind, c],
            recv_sem=self.recv_sem.at[kind, c],
            device_id=(self.p, to),
            device_id_type=MESH,
        )

    def start(self, c):
        for kind in range(4):
            self.copy(kind, c).start()

    def relay(self, c):
        self.copy(0, c).wait_recv()
        self.copy(4, c).start()
        self.copy(1, c).wait_recv()
        self.copy(5, c).start()

    def finish(self, c):
        for kind in (2, 3, 4, 5):
            self.copy(kind, c).wait_recv()

    def drain(self):
        @pl.loop(0, CHUNKS)
        def _(c):
            for kind in range(6):
                self.copy(kind, c).wait_send()


def pipelined(gather, produce, consume):
    @pl.loop(0, CHUNKS)
    def _(c):
        produce(c)
        gather.start(c)

        @pl.when(c >= 1)
        def _():
            gather.relay(c - 1)

        @pl.when(c >= 2)
        def _():
            gather.finish(c - 2)
            consume(c - 2)

    gather.relay(CHUNKS - 1)

    @pl.loop(CHUNKS - 2, CHUNKS)
    def _(c):
        gather.finish(c)
        consume(c)


def conv_project(ext_ref, ext_rows, y_rows, w_ref, first, count, y_ref):
    @pl.loop(0, count // 2)
    def _(j):
        pair = jnp.concatenate([w_ref[first + 2 * j], w_ref[first + 2 * j + 1]], 1)
        y = dot(ext_ref[ext_rows, :], pair).astype(BF)
        y_ref[2 * j, y_rows, :] = y[:, :W]
        y_ref[2 * j + 1, y_rows, :] = y[:, W:]

    if count % 2:
        y = dot(ext_ref[ext_rows, :], w_ref[first + count - 1])
        y_ref[count - 1, y_rows, :] = y.astype(BF)


def conv_select(a, base, nbr_ref, yb_ref, yf_ref):
    start = pl.multiple_of(a * BLK, BLK)
    nbr = jnp.transpose(nbr_ref[:, pl.ds(start, BLK)])
    at = jnp.where(nbr < 0, -4096, nbr - (base + start))
    window = iota((BLK, 2 * BLK), 1)
    acc = yb_ref[MID, pl.ds(start + REACH, BLK), :].astype(F32)
    for t in range(TAPS):
        if t < MID:
            sel = hot(window == at[:, t : t + 1] + REACH)
            acc += dot(sel, yb_ref[t, pl.ds(start, 2 * BLK), :])
        elif t > MID:
            sel = hot(window == at[:, t : t + 1])
            acc += dot(sel, yf_ref[t - MID - 1, pl.ds(start, 2 * BLK), :])
    return acc


def norm_slices(parts, gain_ref):
    mean = sum(jnp.sum(p, 1, keepdims=True) for p in parts) * (1.0 / C)
    centre = [p - mean for p in parts]
    spread = sum(jnp.sum(c * c, 1, keepdims=True) for c in centre) * (1.0 / C)
    scale = lax.rsqrt(spread + 1e-05)
    return [c * scale * gain_ref[:, W * k : W * k + W] for k, c in enumerate(centre)]


def mid_block(a, conv_ref, ext_ref, cpe_ref, n1_ref, h1_ref, normed_ref):
    rows = block(a)
    feats = ext_ref[pl.ds(pl.multiple_of(a * BLK + REACH, BLK), BLK), :].astype(F32)
    normed = norm_slices([conv_ref[k, rows, :].astype(F32) for k in range(HEADS)], cpe_ref)
    h1 = [feats[:, W * k : W * k + W] + normed[k] for k in range(HEADS)]
    for k, part in enumerate(norm_slices(h1, n1_ref)):
        h1_ref[rows, W * k : W * k + W] = h1[k]
        normed_ref[k, rows, :] = part.astype(BF)


def column_of(row):
    same = iota((W, W), 0) == iota((W, W), 1)
    parts = [
        jnp.sum(jnp.where(same, row[:, k : k + W], 0), 1, keepdims=True)
        for k in range(0, row.shape[1], W)
    ]
    return jnp.concatenate(parts, 0)


def bucket_of(rank_row):
    target = rank_row // PTS
    member = iota((DEVS, PTS), 0) == target
    ones = jnp.where(member, 1.0, 0.0)
    upper = hot(iota((PTS, PTS), 0) < iota((PTS, PTS), 1))
    counts = dot(ones.astype(BF), upper)
    slot = jnp.sum(counts * ones, 0, keepdims=True).astype(I32)
    code = rank_row % PTS + 1
    by_slot = hot(iota((W, PTS), 0) == slot)
    high = dot_nt((ones * (code // 32).astype(F32)).astype(BF), by_slot)
    low = dot_nt((ones * (code % 32).astype(F32)).astype(BF), by_slot)
    return target * SLOTS + slot, jnp.concatenate([high, low], 0).astype(BF)


def note_rows(positions):
    r = iota((DEVS * NOTE, W), 0)
    c = iota((DEVS * NOTE, W), 1)
    d = r // NOTE
    place = hot(((r % NOTE == 0) & (c == d)) | ((r % NOTE == 1) & (c == d + DEVS)))
    return dot(place, positions).astype(BF)


def spots_of(notes):
    r = iota((DEVS, DEVS * NOTE), 1)
    q = iota((DEVS, DEVS * NOTE), 0)
    high = dot(hot(r == q * NOTE), notes).astype(BF)
    low = dot(hot(r == q * NOTE + 1), notes).astype(BF)
    pick = hot(iota((W, ROWS), 0) == iota((W, ROWS), 1) % SLOTS)
    full = dot(high, pick) * 32.0 + dot(low, pick) - 1.0
    mine = iota((DEVS, ROWS), 0) == iota((DEVS, ROWS), 1) // SLOTS
    return jnp.sum(jnp.where(mine, full, 0.0), 0, keepdims=True).astype(I32)


def project_qkv(rows, x_ref, wq_ref, wk_ref, wv_ref, qq_ref, k_ref, v_ref):
    def project(w_ref):
        parts = [dot(x_ref[k, rows, :], w_ref[W * k : W * k + W, :]) for k in range(HEADS)]
        return sum(parts).astype(BF)

    scaled = project(wq_ref).astype(F32) * np.float32(np.log2(np.e) / 4.0)
    high = scaled.astype(BF)
    qq_ref[rows, :W] = high
    qq_ref[rows, W:] = (scaled - high.astype(F32)).astype(BF)
    k_ref[rows, :] = project(wk_ref)
    v_ref[rows, :] = project(wv_ref)


def attend(qq_ref, k_ref, v_ref, acc_ref, att_ref):
    acc_ref[...] = jnp.zeros_like(acc_ref)
    lane = iota((PTS, W), 1) // HD

    @pl.loop(0, W // HD)
    def _(head):
        own = lane == head
        zero = jnp.zeros((PTS, W), BF)
        keys = jnp.where(own, k_ref[...], zero)
        keys = jnp.concatenate([keys, keys], 1)
        values = jnp.concatenate([jnp.where(own, v_ref[...], zero), hot(own)], 1)
        for b in range(CHUNKS):
            rows = slice(b * BLK, b * BLK + BLK)
            scores = dot_nt(qq_ref[rows, :], keys)
            top = jnp.max(scores, 1, keepdims=True)
            probs = jnp.exp2(scores - top).astype(BF)
            acc_ref[rows, :] += dot(probs, values)

    att_ref[...] = (acc_ref[:, :W] / acc_ref[:, W:]).astype(BF)


def mlp_block(a, att_ref, h1_ref, wp_ref, n2_ref, f1_ref, f2_ref, out_ref):
    rows = block(a)
    merged = sum(dot(att_ref[k, rows, :], wp_ref[W * k : W * k + W, :]) for k in range(HEADS))
    h2 = h1_ref[rows, :] + merged.astype(BF).astype(F32)
    parts = norm_slices([h2[:, W * k : W * k + W] for k in range(HEADS)], n2_ref)
    normed = jnp.concatenate([part.astype(BF) for part in parts], 1)
    total = h2
    for j in range(MLP // C):
        cols = slice(C * j, C * j + C)
        x = dot(normed, f1_ref[:, cols])
        hidden = (0.5 * x * (1.0 + lax.erf(x * np.float32(np.sqrt(0.5))))).astype(BF)
        total += dot(hidden, f2_ref[cols, :])
    out_ref[rows, :] = total.astype(BF)


def whole_kernel(
    feats_hbm,
    nbr_ref,
    rank_ref,
    cw_hbm,
    cpe_ref,
    n1_ref,
    wq_hbm,
    wk_hbm,
    wv_hbm,
    wp_hbm,
    n2_ref,
    f1_hbm,
    f2_hbm,
    out_hbm,
    ext,
    cw,
    wq,
    wk,
    wv,
    wp,
    f1,
    f2,
    yb,
    yf,
    conv_all,
    placed_all,
    merged_all,
    h1,
    normed,
    note_out,
    note_in,
    there_out,
    there_in,
    back_out,
    back_in,
    to_place,
    from_place,
    from_bucket,
    qq,
    keys,
    values,
    acc,
    att,
    result,
    load_sem,
    halo_send,
    halo_recv,
    block_send,
    block_recv,
    gather_send,
    gather_recv,
    store_sem,
):
    p = lax.axis_index("pts")
    h = lax.axis_index("head")
    loads = [
        pltpu.make_async_copy(source, target, load_sem.at[i])
        for i, (source, target) in enumerate(
            (
                (feats_hbm, ext.at[pl.ds(REACH, PTS)]),
                (cw_hbm, cw),
                (wq_hbm, wq),
                (wk_hbm, wk),
                (wv_hbm, wv),
                (wp_hbm, wp),
                (f1_hbm, f1),
                (f2_hbm, f2),
            )
        )
    ]
    for load in loads:
        load.start()
    barrier_signal(p, h)
    bucket, positions = bucket_of(rank_ref[...])
    note_out[...] = note_rows(positions)
    barrier_wait()

    halos = [
        pltpu.make_async_remote_copy(
            src_ref=feats_hbm.at[pl.ds(first, REACH)],
            dst_ref=ext.at[pl.ds(to, REACH)],
            send_sem=halo_send.at[i],
            recv_sem=halo_recv.at[i],
            device_id=(lax.rem(p + step, DEVS), h),
            device_id_type=MESH,
        )
        for i, (first, to, step) in enumerate(
            ((PTS - REACH, 0, 1), (0, PTS + REACH, DEVS - 1))
        )
    ]
    for halo in halos:
        halo.start()

    @pl.loop(1, DEVS)
    def _(k):
        d = lax.rem(p + k, DEVS)
        send_block(p, h, d, NOTE, note_out, note_in, block_send.at[0], block_recv.at[0])

    note_in[block(p, NOTE), :] = note_out[block(p, NOTE), :]

    loads[0].wait()
    loads[1].wait()
    inner = pl.ds(REACH, PTS)
    conv_project(ext, inner, inner, cw, 0, MID + 1, yb)
    conv_project(ext, inner, pl.ds(0, PTS), cw, MID + 1, MID, yf)
    for halo in halos:
        halo.wait_recv()
    conv_project(ext, pl.ds(0, REACH), pl.ds(0, REACH), cw, 0, MID, yb)
    after = pl.ds(PTS + REACH, REACH)
    conv_project(ext, after, pl.ds(PTS, REACH), cw, MID + 1, MID, yf)

    def convolve(c):
        conv_all[h, block(c), :] = conv_select(c, p * PTS, nbr_ref, yb, yf).astype(BF)

    def norm(c):
        mid_block(c, conv_all, ext, cpe_ref, n1_ref, h1, normed)

    gathers = [
        Gather(p, h, ref, gather_send.at[i], gather_recv.at[i])
        for i, ref in enumerate((conv_all, placed_all, merged_all))
    ]
    pipelined(gathers[0], convolve, norm)

    def scatter(make, out_ref, in_ref, send_sem, recv_sem):
        @pl.loop(0, ROWS // BLK)
        def _(j):
            b = lax.rem(p // GROUP + j, ROWS // BLK)
            out_ref[block(b), :] = make(b).astype(BF)

            @pl.loop(0, GROUP)
            def _(i):
                d = b * GROUP + lax.rem(p + i, GROUP)

                @pl.when(d != p)
                def _():
                    send_block(p, h, d, SLOTS, out_ref, in_ref, send_sem, recv_sem)

        in_ref[block(p, SLOTS), :] = out_ref[block(p, SLOTS), :]

    def pack(b):
        return dot(hot(iota((BLK, PTS), 0) + b * BLK == bucket), normed[h])

    scatter(pack, there_out, there_in, block_send.at[1], block_recv.at[1])
    wait_blocks(NOTE, note_in, block_recv.at[0])
    spots = spots_of(note_in[...])

    @pl.loop(0, CHUNKS)
    def _(c):
        to_place[block(c), :] = hot(iota((BLK, ROWS), 0) + c * BLK == spots)

    spots_column = column_of(spots)
    for k in range(0, ROWS, BLK):
        from_place[k : k + BLK, :] = hot(iota((BLK, PTS), 1) == spots_column[k : k + BLK, :])
    wait_blocks(SLOTS, there_in, block_recv.at[1])
    for load in loads[2:5]:
        load.wait()

    def place(c):
        placed_all[h, block(c), :] = dot(to_place[block(c), :], there_in[...]).astype(BF)

    def project(c):
        project_qkv(block(c), placed_all, wq, wk, wv, qq, keys, values)

    pipelined(gathers[1], place, project)
    attend(qq, keys, values, acc, att)

    def unplace(b):
        return dot(from_place[block(b), :], att[...])

    scatter(unplace, back_out, back_in, block_send.at[2], block_recv.at[2])
    bucket_column = column_of(bucket)
    for k in range(0, PTS, BLK):
        from_bucket[k : k + BLK, :] = hot(iota((BLK, ROWS), 1) == bucket_column[k : k + BLK, :])
    wait_blocks(SLOTS, back_in, block_recv.at[2])
    for load in loads[5:]:
        load.wait()

    def unpack(c):
        merged_all[h, block(c), :] = dot(from_bucket[block(c), :], back_in[...]).astype(BF)

    def store(c):
        return pltpu.make_async_copy(
            result.at[block(c)], out_hbm.at[block(c)], store_sem.at[c]
        )

    def perceive(c):
        mlp_block(c, merged_all, h1, wp, n2_ref, f1, f2, result)
        store(c).start()

    pipelined(gathers[2], unpack, perceive)

    for halo in halos:
        halo.wait_send()
    for i, (size, ref) in enumerate(((NOTE, note_out), (SLOTS, there_out), (SLOTS, back_out))):
        wait_blocks(size, ref, block_send.at[i])
    for gather in gathers:
        gather.drain()

    @pl.loop(0, CHUNKS)
    def _(c):
        store(c).wait()


def per_device(
    feats,
    neighbours,
    rank,
    conv_weight,
    cpe_gain,
    norm1_gain,
    w_query,
    w_key,
    w_value,
    w_proj,
    norm2_gain,
    w_fc1,
    w_fc2,
):
    here, there = pl.BlockSpec(memory_space=VMEM), pl.BlockSpec(memory_space=pl.ANY)
    dma = pltpu.SemaphoreType.DMA
    return pl.pallas_call(
        whole_kernel,
        out_shape=jax.ShapeDtypeStruct((PTS, C), BF),
        in_specs=[there, here, here, there, here, here] + [there] * 4 + [here, there, there],
        out_specs=there,
        scratch_shapes=[
            pltpu.VMEM((PTS + 2 * REACH, C), BF),
            pltpu.VMEM((TAPS, C, W), BF),
            pltpu.VMEM((C, W), BF),
            pltpu.VMEM((C, W), BF),
            pltpu.VMEM((C, W), BF),
            pltpu.VMEM((C, C), BF),
            pltpu.VMEM((C, MLP), BF),
            pltpu.VMEM((MLP, C), BF),
            pltpu.VMEM((MID + 1, PTS + REACH, W), BF),
            pltpu.VMEM((MID, PTS + REACH, W), BF),
            pltpu.VMEM((HEADS, PTS, W), BF),
            pltpu.VMEM((HEADS, PTS, W), BF),
            pltpu.VMEM((HEADS, PTS, W), BF),
            pltpu.VMEM((PTS, C), F32),
            pltpu.VMEM((HEADS, PTS, W), BF),
            pltpu.VMEM((DEVS * NOTE, W), BF),
            pltpu.VMEM((DEVS * NOTE, W), BF),
            pltpu.VMEM((ROWS, W), BF),
            pltpu.VMEM((ROWS, W), BF),
            pltpu.VMEM((ROWS, W), BF),
            pltpu.VMEM((ROWS, W), BF),
            pltpu.VMEM((PTS, ROWS), BF),
            pltpu.VMEM((ROWS, PTS), BF),
            pltpu.VMEM((PTS, ROWS), BF),
            pltpu.VMEM((PTS, 2 * W), BF),
            pltpu.VMEM((PTS, W), BF),
            pltpu.VMEM((PTS, W), BF),
            pltpu.VMEM((PTS, 2 * W), F32),
            pltpu.VMEM((PTS, W), BF),
            pltpu.VMEM((PTS, C), BF),
            dma((8,)),
            dma((2,)),
            dma((2,)),
            dma((3,)),
            dma((3,)),
            dma((3, 6, CHUNKS)),
            dma((3, 6, CHUNKS)),
            dma((CHUNKS,)),
        ],
        compiler_params=pltpu.CompilerParams(
            collective_id=0, has_side_effects=True, vmem_limit_bytes=58 * 2**20
        ),
    )(
        feats,
        neighbours.T,
        rank.reshape(1, PTS),
        conv_weight,
        cpe_gain.reshape(1, C),
        norm1_gain.reshape(1, C),
        w_query,
        w_key,
        w_value,
        w_proj,
        norm2_gain.reshape(1, C),
        w_fc1,
        w_fc2,
    )


def solution(mesh):
    placed = (
        P("pts", None),
        P("pts", None),
        P("pts"),
        P(None, None, "head"),
        P(),
        P(),
        P(None, "head"),
        P(None, "head"),
        P(None, "head"),
        P(),
        P(),
        P(),
        P(),
    )
    return jax.shard_map(
        per_device, mesh=mesh, in_specs=placed, out_specs=P("pts", None), check_vma=False
    )
```

```python
import jax
import jax.numpy as jnp
import numpy as np
from jax import lax
from jax.experimental import pallas as pl
from jax.experimental.pallas import tpu as pltpu
from jax.sharding import PartitionSpec as P

HD = 16
PTS = 1024
REACH = 256
TAPS = 27
MID = 13
C = 512
MLP = 2048
W = 128
HEADS = 4
DEVS = 64
SLOTS = 32
HALF = SLOTS // 2
SIDE = DEVS * HALF
ROWS = DEVS * SLOTS
WAVE = 64
NOTE = 16
BLK = 256
CHUNKS = PTS // BLK
GROUP = BLK // HALF
BF = jnp.bfloat16
F32 = jnp.float32
I32 = jnp.int32
VMEM = pltpu.MemorySpace.VMEM
MESH = pl.DeviceIdType.MESH


def iota(shape, dim):
    return lax.broadcasted_iota(I32, shape, dim)


def dot(a, b):
    return jnp.dot(a, b, preferred_element_type=F32)


def dot_nt(a, b):
    return lax.dot_general(a, b, (((1,), (1,)), ((), ())), preferred_element_type=F32)


def hot(mask):
    return jnp.where(mask, 1.0, 0.0).astype(BF)


def turned(x):
    return pltpu.roll(x.astype(F32), WAVE, 1).astype(x.dtype)


def beside(low, high):
    return jnp.where(iota(low.shape, 1) < WAVE, low, high)


def block(a, size=BLK):
    return pl.ds(pl.multiple_of(a * size, size), size)


def barrier_signal(p, h):
    barrier = pltpu.get_barrier_semaphore()

    @pl.loop(1, DEVS)
    def _(k):
        pl.semaphore_signal(
            barrier, inc=1, device_id=(lax.rem(p + k, DEVS), h), device_id_type=MESH
        )

    for k in (1, HEADS - 1):
        pl.semaphore_signal(
            barrier, inc=1, device_id=(p, lax.rem(h + k, HEADS)), device_id_type=MESH
        )


def barrier_wait():
    pl.semaphore_wait(pltpu.get_barrier_semaphore(), DEVS + 1)


def send_block(p, h, d, size, out_ref, in_ref, send_sem, recv_sem):
    pltpu.make_async_remote_copy(
        src_ref=out_ref.at[block(d, size)],
        dst_ref=in_ref.at[block(p, size)],
        send_sem=send_sem,
        recv_sem=recv_sem,
        device_id=(d, h),
        device_id_type=MESH,
    ).start()


def wait_blocks(size, ref, sem):
    part = ref.at[pl.ds(0, (DEVS - 1) * size)]
    pltpu.make_async_copy(part, part, sem).wait()


class Gather:
    def __init__(self, p, h, ref, send_sem, recv_sem):
        self.p, self.h, self.ref, self.send_sem, self.recv_sem = p, h, ref, send_sem, recv_sem
        self.right, self.left = lax.rem(h + 1, HEADS), lax.rem(h + 3, HEADS)
        self.half = ref.shape[1] // CHUNKS // 2

    def copy(self, kind, c):
        owner, upper, to = (
            (self.h, True, self.right),
            (self.h, False, self.left),
            (self.h, False, self.right),
            (self.h, True, self.left),
            (self.left, True, self.right),
            (self.right, False, self.left),
        )[kind]
        start = pl.multiple_of((2 * c + (0 if upper else 1)) * self.half, self.half)
        rows = self.ref.at[owner, pl.ds(start, self.half)]
        return pltpu.make_async_remote_copy(
            src_ref=rows,
            dst_ref=rows,
            send_sem=self.send_sem.at[kind, c],
            recv_sem=self.recv_sem.at[kind, c],
            device_id=(self.p, to),
            device_id_type=MESH,
        )

    def start(self, c):
        for kind in range(4):
            self.copy(kind, c).start()

    def relay(self, c):
        self.copy(0, c).wait_recv()
        self.copy(4, c).start()
        self.copy(1, c).wait_recv()
        self.copy(5, c).start()

    def finish(self, c):
        for kind in (2, 3, 4, 5):
            self.copy(kind, c).wait_recv()

    def drain(self):
        @pl.loop(0, CHUNKS)
        def _(c):
            for kind in range(6):
                self.copy(kind, c).wait_send()


def conv_project(ext_ref, ext_rows, y_rows, w_ref, first, count, y_ref):
    for j in range(0, count, 2):
        if j + 1 < count:
            pair = jnp.concatenate([w_ref[first + j], w_ref[first + j + 1]], 1)
            y = dot(ext_ref[ext_rows, :], pair).astype(BF)
            y_ref[j, y_rows, :] = y[:, :W]
            y_ref[j + 1, y_rows, :] = y[:, W:]
        else:
            y_ref[j, y_rows, :] = dot(ext_ref[ext_rows, :], w_ref[first + j]).astype(BF)


def conv_select(a, base, nbr_ref, yb_ref, yf_ref):
    start = pl.multiple_of(a * BLK, BLK)
    nbr = jnp.transpose(nbr_ref[:, pl.ds(start, BLK)])
    at = jnp.where(nbr < 0, -4096, nbr - (base + start))
    window = iota((BLK, 2 * BLK), 1)
    acc = yb_ref[MID, pl.ds(start + REACH, BLK), :].astype(F32)
    for t in range(TAPS):
        if t < MID:
            sel = hot(window == at[:, t : t + 1] + REACH)
            acc += dot(sel, yb_ref[t, pl.ds(start, 2 * BLK), :])
        elif t > MID:
            sel = hot(window == at[:, t : t + 1])
            acc += dot(sel, yf_ref[t - MID - 1, pl.ds(start, 2 * BLK), :])
    return acc


def norm_slices(parts, gain_ref):
    mean = sum(jnp.sum(p, 1, keepdims=True) for p in parts) * (1.0 / C)
    centre = [p - mean for p in parts]
    spread = sum(jnp.sum(c * c, 1, keepdims=True) for c in centre) * (1.0 / C)
    scale = lax.rsqrt(spread + 1e-05)
    return [c * scale * gain_ref[:, W * k : W * k + W] for k, c in enumerate(centre)]


def mid_block(a, conv_ref, ext_ref, cpe_ref, n1_ref, h1_ref, normed_ref):
    rows = block(a)
    feats = ext_ref[pl.ds(pl.multiple_of(a * BLK + REACH, BLK), BLK), :].astype(F32)
    normed = norm_slices([conv_ref[k, rows, :].astype(F32) for k in range(HEADS)], cpe_ref)
    h1 = [feats[:, W * k : W * k + W] + normed[k] for k in range(HEADS)]
    for k, part in enumerate(norm_slices(h1, n1_ref)):
        h1_ref[rows, W * k : W * k + W] = h1[k]
        normed_ref[k, rows, :] = part.astype(BF)


def column_of(row):
    same = iota((W, W), 0) == iota((W, W), 1)
    parts = [
        jnp.sum(jnp.where(same, row[:, k : k + W], 0), 1, keepdims=True)
        for k in range(0, row.shape[1], W)
    ]
    return jnp.concatenate(parts, 0)


def bucket_of(rank_row):
    target = rank_row // PTS
    member = iota((DEVS, PTS), 0) == target
    ones = jnp.where(member, 1.0, 0.0)
    upper = hot(iota((PTS, PTS), 0) < iota((PTS, PTS), 1))
    counts = dot(ones.astype(BF), upper)
    slot = jnp.sum(counts * ones, 0, keepdims=True).astype(I32)
    code = rank_row % PTS + 1
    by_slot = hot(iota((W, PTS), 0) == slot)
    high = dot_nt((ones * (code // 32).astype(F32)).astype(BF), by_slot)
    low = dot_nt((ones * (code % 32).astype(F32)).astype(BF), by_slot)
    row = slot // HALF * SIDE + target * HALF + slot % HALF
    return row, jnp.concatenate([high, low], 0).astype(BF)


def note_rows(positions):
    r = iota((DEVS * NOTE, W), 0)
    c = iota((DEVS * NOTE, W), 1)
    d = r // NOTE
    place = hot(((r % NOTE == 0) & (c == d)) | ((r % NOTE == 1) & (c == d + DEVS)))
    return dot(place, positions).astype(BF)


def spots_of(notes):
    r = iota((DEVS, DEVS * NOTE), 1)
    q = iota((DEVS, DEVS * NOTE), 0)
    high = dot(hot(r == q * NOTE), notes).astype(BF)
    low = dot(hot(r == q * NOTE + 1), notes).astype(BF)
    row = iota((W, ROWS), 1)
    pick = hot(iota((W, ROWS), 0) == row // SIDE * HALF + row % HALF)
    full = dot(high, pick) * 32.0 + dot(low, pick) - 1.0
    mine = iota((DEVS, ROWS), 0) == iota((DEVS, ROWS), 1) % SIDE // HALF
    return jnp.sum(jnp.where(mine, full, 0.0), 0, keepdims=True).astype(I32)


def joined(c, ref):
    rows = block(c, BLK // 2)
    parts = []
    for k in range(HEADS):
        first, last = ref[0, k, rows, :], ref[1, k, rows, :]
        parts.append(
            jnp.concatenate([beside(first, turned(last)), beside(turned(first), last)], 0)
        )
    return jnp.concatenate(parts, 1)


def project_qkv(c, x_ref, w_ref, qq_ref, k_ref, v_ref):
    rows = block(c)
    qkv = dot(joined(c, x_ref), w_ref[...]).astype(BF)
    scaled = qkv[:, :W].astype(F32) * np.float32(np.log2(np.e) / 4.0)
    high = scaled.astype(BF)
    qq_ref[rows, :W] = high
    qq_ref[rows, W:] = (scaled - high.astype(F32)).astype(BF)
    k_ref[rows, :] = qkv[:, W : 2 * W]
    v_ref[rows, :] = qkv[:, 2 * W :]


def attend(wave, qq_ref, k_ref, v_ref, acc_ref, att_ref):
    acc_ref[...] = jnp.zeros_like(acc_ref)
    lane = iota((PTS, W), 1) // HD
    heads = WAVE // HD

    def operands(head):
        own = lane == head
        zero = jnp.zeros((PTS, W), BF)
        keys = jnp.where(own, k_ref[...], zero)
        values = jnp.where(own, v_ref[...], zero)
        return jnp.concatenate([keys, keys], 1), jnp.concatenate([values, hot(own)], 1)

    @pl.loop(wave * heads, wave * heads + heads, step=2)
    def _(first):
        pairs = [operands(first), operands(first + 1)]
        steps = [(pair, slice(b * BLK, b * BLK + BLK)) for pair in pairs for b in range(CHUNKS)]
        coming = dot_nt(qq_ref[steps[0][1], :], steps[0][0][0])
        for i, ((_, values), rows) in enumerate(steps):
            scores = coming
            if i + 1 < len(steps):
                (keys, _), later = steps[i + 1]
                coming = dot_nt(qq_ref[later, :], keys)
            top = jnp.max(scores, 1, keepdims=True)
            probs = jnp.exp2(scores - top).astype(BF)
            acc_ref[rows, :] += dot(probs, values)

    done = lane // heads == wave
    straight = jnp.where(done, acc_ref[:, :W] / jnp.where(done, acc_ref[:, W:], 1.0), 0.0)
    other = pltpu.roll(straight, WAVE, 1)
    first, last = (other, straight) if wave else (straight, other)
    att_ref[:, :W] = first.astype(BF)
    att_ref[:, W:] = last.astype(BF)


def gelu(x):
    return 0.5 * x * (1.0 + lax.erf(x * np.float32(np.sqrt(0.5))))


def mlp_rows(a, att_ref, h1_ref, wp_ref, n2_ref):
    merged = dot(joined(a, att_ref), wp_ref[...])
    h2 = h1_ref[block(a), :] + merged.astype(BF).astype(F32)
    parts = norm_slices([h2[:, W * k : W * k + W] for k in range(HEADS)], n2_ref)
    return h2, jnp.concatenate([part.astype(BF) for part in parts], 1)


def mlp_blocks(chunks, att_ref, h1_ref, wp_ref, n2_ref, f1_ref, f2_ref, out_ref):
    width = C // 2
    steps = [(i, slice(j, j + width)) for i in range(len(chunks)) for j in range(0, MLP, width)]
    ready = [mlp_rows(chunks[0], att_ref, h1_ref, wp_ref, n2_ref)]
    total = [ready[0][0]]
    coming = dot(ready[0][1], f1_ref[:, steps[0][1]])
    for n, (i, cols) in enumerate(steps):
        x = coming
        if n + 3 < len(steps) and steps[n + 3][0] == len(ready):
            ready.append(mlp_rows(chunks[len(ready)], att_ref, h1_ref, wp_ref, n2_ref))
            total.append(ready[-1][0])
        if n + 1 < len(steps):
            later, ahead = steps[n + 1]
            coming = dot(ready[later][1], f1_ref[:, ahead])
        total[i] += dot(gelu(x).astype(BF), f2_ref[cols, :])
        if cols.stop == MLP:
            out_ref[block(chunks[i]), :] = total[i].astype(BF)


def whole_kernel(
    feats_hbm,
    nbr_ref,
    rank_ref,
    cw_hbm,
    cpe_ref,
    n1_ref,
    wq_hbm,
    wk_hbm,
    wv_hbm,
    wp_hbm,
    n2_ref,
    f1_hbm,
    f2_hbm,
    out_hbm,
    ext,
    cw,
    wqkv,
    wp,
    f1,
    f2,
    yb,
    yf,
    conv_all,
    placed_all,
    merged_all,
    h1,
    normed,
    note_out,
    note_in,
    there_out,
    there_in,
    back_out,
    back_in,
    to_place,
    from_place,
    from_bucket,
    qq,
    keys,
    values,
    acc,
    att,
    result,
    load_sem,
    halo_send,
    halo_recv,
    block_send,
    block_recv,
    gather_send,
    gather_recv,
    store_sem,
):
    p = lax.axis_index("pts")
    h = lax.axis_index("head")
    loads = [
        pltpu.make_async_copy(source, target, load_sem.at[i])
        for i, (source, target) in enumerate(
            (
                (feats_hbm, ext.at[pl.ds(REACH, PTS)]),
                (cw_hbm, cw),
                (wq_hbm, wqkv.at[:, pl.ds(0, W)]),
                (wk_hbm, wqkv.at[:, pl.ds(W, W)]),
                (wv_hbm, wqkv.at[:, pl.ds(2 * W, W)]),
                (wp_hbm, wp),
                (f1_hbm, f1),
                (f2_hbm, f2),
            )
        )
    ]
    for load in loads:
        load.start()
    barrier_signal(p, h)
    bucket, positions = bucket_of(rank_ref[...])
    note_out[...] = note_rows(positions)
    loads[0].wait()
    loads[1].wait()
    inner = pl.ds(REACH, PTS)
    conv_project(ext, inner, inner, cw, 0, MID + 1, yb)
    barrier_wait()

    halos = [
        pltpu.make_async_remote_copy(
            src_ref=feats_hbm.at[pl.ds(first, REACH)],
            dst_ref=ext.at[pl.ds(to, REACH)],
            send_sem=halo_send.at[i],
            recv_sem=halo_recv.at[i],
            device_id=(lax.rem(p + step, DEVS), h),
            device_id_type=MESH,
        )
        for i, (first, to, step) in enumerate(
            ((PTS - REACH, 0, 1), (0, PTS + REACH, DEVS - 1))
        )
    ]
    for halo in halos:
        halo.start()
    conv_project(ext, inner, pl.ds(0, PTS), cw, MID + 1, MID, yf)

    gathers = [
        Gather(p, h, ref, gather_send.at[i], gather_recv.at[i])
        for i, ref in enumerate(
            [conv_all] + [ref.at[w] for ref in (placed_all, merged_all) for w in range(2)]
        )
    ]
    gather = gathers[0]

    def convolve(c):
        conv_all[h, block(c), :] = conv_select(c, p * PTS, nbr_ref, yb, yf).astype(BF)
        gather.start(c)

    def norm(c):
        gather.finish(c)
        mid_block(c, conv_all, ext, cpe_ref, n1_ref, h1, normed)

    @pl.loop(1, 3)
    def _(c):
        convolve(c)

    for halo in halos:
        halo.wait_recv()

    @pl.loop(1, DEVS)
    def _(k):
        d = lax.rem(p + k, DEVS)
        send_block(p, h, d, NOTE, note_out, note_in, block_send.at[0], block_recv.at[0])

    note_in[block(p, NOTE), :] = note_out[block(p, NOTE), :]

    conv_project(ext, pl.ds(0, REACH), pl.ds(0, REACH), cw, 0, MID, yb)
    after = pl.ds(PTS + REACH, REACH)
    conv_project(ext, after, pl.ds(PTS, REACH), cw, MID + 1, MID, yf)
    gather.relay(1)
    gather.relay(2)

    @pl.loop(0, 2)
    def _(j):
        convolve(3 * j)
        norm(1 + j)

    gather.relay(0)
    gather.relay(3)
    norm(0)
    norm(3)

    x, z, core = p // GROUP, lax.rem(p, GROUP) // 2, lax.rem(p, 2)

    def send_wave(w, b, out_ref, in_ref, i):
        def send(d):
            send_block(
                p, h, d, HALF, out_ref.at[w], in_ref.at[w],
                block_send.at[i + w], block_recv.at[i + w],
            )

        for ahead in (4, 3, 5, 2, 6, 1, 7):
            chip = b * GROUP + 2 * lax.rem(z + ahead, GROUP // 2)
            send(chip)
            send(chip + 1)
        chip = b * GROUP + 2 * z
        send(chip + 1 - core)

        @pl.when(b != x)
        def _():
            send(chip + core)

    def turn_of(j):
        return lax.rem(x + 2 + 3 * j, CHUNKS)

    def keep_own(w, out_ref, in_ref):
        in_ref[w, block(p, HALF), :] = out_ref[w, block(p, HALF), :]

    own = normed[h]
    own = jnp.concatenate([own, turned(own)], 1)

    @pl.loop(0, CHUNKS)
    def _(j):
        b = turn_of(j)
        row = iota((BLK, PTS), 0) + b * BLK
        low = dot(hot(row == bucket), own)
        high = dot(hot(row + SIDE == bucket), own)
        there_out[0, block(b), :] = beside(low[:, :W], high[:, W:]).astype(BF)
        there_out[1, block(b), :] = beside(low[:, W:], high[:, :W]).astype(BF)
        send_wave(0, b, there_out, there_in, 1)

    @pl.loop(0, CHUNKS)
    def _(j):
        send_wave(1, turn_of(j), there_out, there_in, 1)

    for w in range(2):
        keep_own(w, there_out, there_in)
    wait_blocks(NOTE, note_in, block_recv.at[0])
    spots = spots_of(note_in[...])

    @pl.loop(0, CHUNKS)
    def _(c):
        to_place[block(c), :] = hot(iota((BLK, ROWS), 0) + c * BLK == spots)

    def unbundle(w, in_ref, i, chosen, all_ref, gather, earlier=None):
        wait_blocks(HALF, in_ref.at[w], block_recv.at[i + w])
        half = BLK // 2
        for c in range(CHUNKS):
            low = dot(chosen[block(c), :SIDE], in_ref[w])
            high = dot(chosen[block(c), SIDE:], in_ref[w])
            first = low[:half] + pltpu.roll(high[:half], WAVE, 1)
            last = pltpu.roll(low[half:], WAVE, 1) + high[half:]
            all_ref[w, h, block(c, half), :] = beside(first, last).astype(BF)
            gather.start(c)
            if earlier is not None:
                earlier.relay(c)

    def relay(gather):
        @pl.loop(0, CHUNKS)
        def _(c):
            gather.relay(c)

    unbundle(0, there_in, 1, to_place, placed_all, gathers[1])
    spots_column = column_of(spots)
    for k in range(0, ROWS, BLK):
        from_place[k : k + BLK, :] = hot(iota((BLK, PTS), 1) == spots_column[k : k + BLK, :])
    unbundle(1, there_in, 1, to_place, placed_all, gathers[2], gathers[1])
    bucket_column = column_of(bucket)
    for k in range(0, PTS, BLK):
        from_bucket[k : k + BLK, :] = hot(iota((BLK, ROWS), 1) == bucket_column[k : k + BLK, :])
    relay(gathers[2])
    for load in loads[2:5]:
        load.wait()

    @pl.loop(0, CHUNKS)
    def _(c):
        gathers[1].finish(c)
        gathers[2].finish(c)
        project_qkv(c, placed_all, wqkv, qq, keys, values)

    for w in range(2):
        attend(w, qq, keys, values, acc, att)

        @pl.loop(0, CHUNKS)
        def _(j):
            b = turn_of(j)
            low = dot(from_place[block(b), :], att[...])
            high = dot(from_place[block(b + CHUNKS), :], att[...])
            back_out[w, block(b), :] = beside(low[:, :W], high[:, W:]).astype(BF)
            send_wave(w, b, back_out, back_in, 3)

        keep_own(w, back_out, back_in)

    unbundle(0, back_in, 3, from_bucket, merged_all, gathers[3])
    relay(gathers[3])
    unbundle(1, back_in, 3, from_bucket, merged_all, gathers[4])
    relay(gathers[4])
    for load in loads[5:]:
        load.wait()

    def store(c):
        rows = block(c, 2 * BLK)
        return pltpu.make_async_copy(result.at[rows], out_hbm.at[rows], store_sem.at[c])

    @pl.loop(0, CHUNKS, step=2)
    def _(c):
        for k in range(2):
            gathers[3].finish(c + k)
            gathers[4].finish(c + k)
        mlp_blocks([c, c + 1], merged_all, h1, wp, n2_ref, f1, f2, result)
        store(c // 2).start()

    for halo in halos:
        halo.wait_send()
    wait_blocks(NOTE, note_out, block_send.at[0])
    for w in range(2):
        wait_blocks(HALF, there_out.at[w], block_send.at[1 + w])
        wait_blocks(HALF, back_out.at[w], block_send.at[3 + w])
    for gather in gathers:
        gather.drain()
    for c in range(2):
        store(c).wait()


def per_device(
    feats,
    neighbours,
    rank,
    conv_weight,
    cpe_gain,
    norm1_gain,
    w_query,
    w_key,
    w_value,
    w_proj,
    norm2_gain,
    w_fc1,
    w_fc2,
):
    here, there = pl.BlockSpec(memory_space=VMEM), pl.BlockSpec(memory_space=pl.ANY)
    dma = pltpu.SemaphoreType.DMA
    return pl.pallas_call(
        whole_kernel,
        out_shape=jax.ShapeDtypeStruct((PTS, C), BF),
        in_specs=[there, here, here, there, here, here] + [there] * 4 + [here, there, there],
        out_specs=there,
        scratch_shapes=[
            pltpu.VMEM((PTS + 2 * REACH, C), BF),
            pltpu.VMEM((TAPS, C, W), BF),
            pltpu.VMEM((C, 3 * W), BF),
            pltpu.VMEM((C, C), BF),
            pltpu.VMEM((C, MLP), BF),
            pltpu.VMEM((MLP, C), BF),
            pltpu.VMEM((MID + 1, PTS + REACH, W), BF),
            pltpu.VMEM((MID, PTS + REACH, W), BF),
            pltpu.VMEM((HEADS, PTS, W), BF),
            pltpu.VMEM((2, HEADS, PTS // 2, W), BF),
            pltpu.VMEM((2, HEADS, PTS // 2, W), BF),
            pltpu.VMEM((PTS, C), F32),
            pltpu.VMEM((HEADS, PTS, W), BF),
            pltpu.VMEM((DEVS * NOTE, W), BF),
            pltpu.VMEM((DEVS * NOTE, W), BF),
            pltpu.VMEM((2, SIDE, W), BF),
            pltpu.VMEM((2, SIDE, W), BF),
            pltpu.VMEM((2, SIDE, W), BF),
            pltpu.VMEM((2, SIDE, W), BF),
            pltpu.VMEM((PTS, ROWS), BF),
            pltpu.VMEM((ROWS, PTS), BF),
            pltpu.VMEM((PTS, ROWS), BF),
            pltpu.VMEM((PTS, 2 * W), BF),
            pltpu.VMEM((PTS, W), BF),
            pltpu.VMEM((PTS, W), BF),
            pltpu.VMEM((PTS, 2 * W), F32),
            pltpu.VMEM((PTS, 2 * W), BF),
            pltpu.VMEM((PTS, C), BF),
            dma((8,)),
            dma((2,)),
            dma((2,)),
            dma((5,)),
            dma((5,)),
            dma((5, 6, CHUNKS)),
            dma((5, 6, CHUNKS)),
            dma((2,)),
        ],
        compiler_params=pltpu.CompilerParams(
            collective_id=0, has_side_effects=True, vmem_limit_bytes=58 * 2**20
        ),
    )(
        feats,
        neighbours.T,
        rank.reshape(1, PTS),
        conv_weight,
        cpe_gain.reshape(1, C),
        norm1_gain.reshape(1, C),
        w_query,
        w_key,
        w_value,
        w_proj,
        norm2_gain.reshape(1, C),
        w_fc1,
        w_fc2,
    )


def solution(mesh):
    placed = (
        P("pts", None),
        P("pts", None),
        P("pts"),
        P(None, None, "head"),
        P(),
        P(),
        P(None, "head"),
        P(None, "head"),
        P(None, "head"),
        P(),
        P(),
        P(),
        P(),
    )
    return jax.shard_map(
        per_device, mesh=mesh, in_specs=placed, out_specs=P("pts", None), check_vma=False
    )
```

```python
import jax
import jax.numpy as jnp
import numpy as np
from jax import lax
from jax.experimental import pallas as pl
from jax.experimental.pallas import tpu as pltpu
from jax.sharding import PartitionSpec as P

HD = 16
PTS = 1024
REACH = 256
TAPS = 27
MID = 13
C = 512
MLP = 2048
W = 128
HEADS = 4
DEVS = 64
SLOTS = 32
HALF = SLOTS // 2
SIDE = DEVS * HALF
ROWS = DEVS * SLOTS
WAVE = 64
NOTE = 16
BLK = 256
CHUNKS = PTS // BLK
GROUP = BLK // HALF
BF = jnp.bfloat16
F32 = jnp.float32
I32 = jnp.int32
VMEM = pltpu.MemorySpace.VMEM
MESH = pl.DeviceIdType.MESH


def iota(shape, dim):
    return lax.broadcasted_iota(I32, shape, dim)


def dot(a, b):
    return jnp.dot(a, b, preferred_element_type=F32)


def dot_nt(a, b):
    return lax.dot_general(a, b, (((1,), (1,)), ((), ())), preferred_element_type=F32)


def hot(mask):
    return jnp.where(mask, 1.0, 0.0).astype(BF)


def turned(x):
    return pltpu.roll(x.astype(F32), WAVE, 1).astype(x.dtype)


def beside(low, high):
    return jnp.where(iota(low.shape, 1) < WAVE, low, high)


def block(a, size=BLK):
    return pl.ds(pl.multiple_of(a * size, size), size)


def barrier_signal(p, h):
    barrier = pltpu.get_barrier_semaphore()

    @pl.loop(1, DEVS)
    def _(k):
        pl.semaphore_signal(
            barrier, inc=1, device_id=(lax.rem(p + k, DEVS), h), device_id_type=MESH
        )

    for k in range(1, HEADS):
        pl.semaphore_signal(
            barrier, inc=1, device_id=(p, lax.rem(h + k, HEADS)), device_id_type=MESH
        )


def barrier_wait():
    pl.semaphore_wait(pltpu.get_barrier_semaphore(), DEVS - 1 + HEADS - 1)


def send_block(p, h, d, size, out_ref, in_ref, send_sem, recv_sem):
    pltpu.make_async_remote_copy(
        src_ref=out_ref.at[block(d, size)],
        dst_ref=in_ref.at[block(p, size)],
        send_sem=send_sem,
        recv_sem=recv_sem,
        device_id=(d, h),
        device_id_type=MESH,
    ).start()


def wait_blocks(size, ref, sem):
    part = ref.at[pl.ds(0, (DEVS - 1) * size)]
    pltpu.make_async_copy(part, part, sem).wait()


class Gather:
    def __init__(self, p, h, ref, send_sem, recv_sem):
        self.p, self.h, self.ref, self.send_sem, self.recv_sem = p, h, ref, send_sem, recv_sem
        self.size = ref.shape[1] // CHUNKS

    def copy(self, step, c, owner):
        rows = self.ref.at[owner, block(c, self.size)]
        return pltpu.make_async_remote_copy(
            src_ref=rows,
            dst_ref=rows,
            send_sem=self.send_sem.at[step - 1, c],
            recv_sem=self.recv_sem.at[step - 1, c],
            device_id=(self.p, lax.rem(self.h + step, HEADS)),
            device_id_type=MESH,
        )

    def start(self, c):
        for step in (2, 1, 3):
            self.copy(step, c, self.h).start()

    def finish(self, c):
        for step in (1, 3, 2):
            self.copy(step, c, lax.rem(self.h + HEADS - step, HEADS)).wait_recv()

    def drain(self):
        @pl.loop(0, CHUNKS)
        def _(c):
            for step in (1, 2, 3):
                self.copy(step, c, self.h).wait_send()


def conv_project(ext_ref, ext_rows, y_rows, w_ref, first, count, y_ref):
    for j in range(0, count, 2):
        if j + 1 < count:
            pair = jnp.concatenate([w_ref[first + j], w_ref[first + j + 1]], 1)
            y = dot(ext_ref[ext_rows, :], pair).astype(BF)
            y_ref[j, y_rows, :] = y[:, :W]
            y_ref[j + 1, y_rows, :] = y[:, W:]
        else:
            y_ref[j, y_rows, :] = dot(ext_ref[ext_rows, :], w_ref[first + j]).astype(BF)


def conv_select(a, base, nbr_ref, yb_ref, yf_ref):
    start = pl.multiple_of(a * BLK, BLK)
    nbr = jnp.transpose(nbr_ref[:, pl.ds(start, BLK)])
    at = jnp.where(nbr < 0, -4096, nbr - (base + start))
    window = iota((BLK, 2 * BLK), 1)
    acc = yb_ref[MID, pl.ds(start + REACH, BLK), :].astype(F32)
    for t in range(TAPS):
        if t < MID:
            sel = hot(window == at[:, t : t + 1] + REACH)
            acc += dot(sel, yb_ref[t, pl.ds(start, 2 * BLK), :])
        elif t > MID:
            sel = hot(window == at[:, t : t + 1])
            acc += dot(sel, yf_ref[t - MID - 1, pl.ds(start, 2 * BLK), :])
    return acc


def norm_slices(parts, gain_ref):
    mean = sum(jnp.sum(p, 1, keepdims=True) for p in parts) * (1.0 / C)
    centre = [p - mean for p in parts]
    spread = sum(jnp.sum(c * c, 1, keepdims=True) for c in centre) * (1.0 / C)
    scale = lax.rsqrt(spread + 1e-05)
    return [c * scale * gain_ref[:, W * k : W * k + W] for k, c in enumerate(centre)]


def mid_block(a, conv_ref, ext_ref, cpe_ref, n1_ref, h1_ref, normed_ref):
    rows = block(a)
    feats = ext_ref[pl.ds(pl.multiple_of(a * BLK + REACH, BLK), BLK), :].astype(F32)
    normed = norm_slices([conv_ref[k, rows, :].astype(F32) for k in range(HEADS)], cpe_ref)
    h1 = [feats[:, W * k : W * k + W] + normed[k] for k in range(HEADS)]
    for k, part in enumerate(norm_slices(h1, n1_ref)):
        h1_ref[rows, W * k : W * k + W] = h1[k]
        normed_ref[k, rows, :] = part.astype(BF)


def column_of(row):
    same = iota((W, W), 0) == iota((W, W), 1)
    parts = [
        jnp.sum(jnp.where(same, row[:, k : k + W], 0), 1, keepdims=True)
        for k in range(0, row.shape[1], W)
    ]
    return jnp.concatenate(parts, 0)


def bucket_of(rank_row):
    target = rank_row // PTS
    member = iota((DEVS, PTS), 0) == target
    ones = jnp.where(member, 1.0, 0.0)
    upper = hot(iota((PTS, PTS), 0) < iota((PTS, PTS), 1))
    counts = dot(ones.astype(BF), upper)
    slot = jnp.sum(counts * ones, 0, keepdims=True).astype(I32)
    code = rank_row % PTS + 1
    by_slot = hot(iota((W, PTS), 0) == slot)
    high = dot_nt((ones * (code // 32).astype(F32)).astype(BF), by_slot)
    low = dot_nt((ones * (code % 32).astype(F32)).astype(BF), by_slot)
    row = slot // HALF * SIDE + target * HALF + slot % HALF
    return row, jnp.concatenate([high, low], 0).astype(BF)


def note_rows(positions):
    r = iota((DEVS * NOTE, W), 0)
    c = iota((DEVS * NOTE, W), 1)
    d = r // NOTE
    place = hot(((r % NOTE == 0) & (c == d)) | ((r % NOTE == 1) & (c == d + DEVS)))
    return dot(place, positions).astype(BF)


def spots_of(notes):
    r = iota((DEVS, DEVS * NOTE), 1)
    q = iota((DEVS, DEVS * NOTE), 0)
    high = dot(hot(r == q * NOTE), notes).astype(BF)
    low = dot(hot(r == q * NOTE + 1), notes).astype(BF)
    row = iota((W, ROWS), 1)
    pick = hot(iota((W, ROWS), 0) == row // SIDE * HALF + row % HALF)
    full = dot(high, pick) * 32.0 + dot(low, pick) - 1.0
    mine = iota((DEVS, ROWS), 0) == iota((DEVS, ROWS), 1) % SIDE // HALF
    return jnp.sum(jnp.where(mine, full, 0.0), 0, keepdims=True).astype(I32)


def joined(c, ref):
    rows = block(c, BLK // 2)
    parts = []
    for k in range(HEADS):
        first, last = ref[0, k, rows, :], ref[1, k, rows, :]
        parts.append(
            jnp.concatenate([beside(first, turned(last)), beside(turned(first), last)], 0)
        )
    return jnp.concatenate(parts, 1)


def project_qkv(c, x_ref, w_ref, qq_ref, k_ref, v_ref):
    rows = block(c)
    qkv = dot(joined(c, x_ref), w_ref[...]).astype(BF)
    scaled = qkv[:, :W].astype(F32) * np.float32(np.log2(np.e) / 4.0)
    high = scaled.astype(BF)
    qq_ref[rows, :W] = high
    qq_ref[rows, W:] = (scaled - high.astype(F32)).astype(BF)
    k_ref[rows, :] = qkv[:, W : 2 * W]
    v_ref[rows, :] = qkv[:, 2 * W :]


def attend(wave, qq_ref, k_ref, v_ref, acc_ref, att_ref):
    acc_ref[...] = jnp.zeros_like(acc_ref)
    lane = iota((PTS, W), 1) // HD
    heads = WAVE // HD

    def operands(head):
        own = lane == head
        zero = jnp.zeros((PTS, W), BF)
        keys = jnp.where(own, k_ref[...], zero)
        values = jnp.where(own, v_ref[...], zero)
        return jnp.concatenate([keys, keys], 1), jnp.concatenate([values, hot(own)], 1)

    @pl.loop(wave * heads, wave * heads + heads, step=2)
    def _(first):
        pairs = [operands(first), operands(first + 1)]
        steps = [(pair, slice(b, b + BLK)) for pair in pairs for b in range(0, PTS, BLK)]
        coming = dot_nt(qq_ref[steps[0][1], :], steps[0][0][0])
        for i, ((_, values), rows) in enumerate(steps):
            scores = coming
            if i + 1 < len(steps):
                (keys, _), later = steps[i + 1]
                coming = dot_nt(qq_ref[later, :], keys)
            top = jnp.max(scores, 1, keepdims=True)
            probs = jnp.exp2(scores - top).astype(BF)
            acc_ref[rows, :] += dot(probs, values)

    done = lane // heads == wave
    straight = jnp.where(done, acc_ref[:, :W] / jnp.where(done, acc_ref[:, W:], 1.0), 0.0)
    other = pltpu.roll(straight, WAVE, 1)
    first, last = (other, straight) if wave else (straight, other)
    att_ref[:, :W] = first.astype(BF)
    att_ref[:, W:] = last.astype(BF)


def gelu(x):
    return 0.5 * x * (1.0 + lax.erf(x * np.float32(np.sqrt(0.5))))


def mlp_rows(a, att_ref, h1_ref, wp_ref, n2_ref):
    merged = dot(joined(a, att_ref), wp_ref[...])
    h2 = h1_ref[block(a), :] + merged.astype(BF).astype(F32)
    parts = norm_slices([h2[:, W * k : W * k + W] for k in range(HEADS)], n2_ref)
    return h2, jnp.concatenate([part.astype(BF) for part in parts], 1)


def mlp_blocks(finish, done, att_ref, h1_ref, wp_ref, n2_ref, f1_ref, f2_ref, out_ref):
    width = C // 2
    steps = [(i, slice(j, j + width)) for i in range(CHUNKS) for j in range(0, MLP, width)]
    ready, total = [], []

    def prepare(c):
        finish(c)
        ready.append(mlp_rows(c, att_ref, h1_ref, wp_ref, n2_ref))
        total.append(ready[-1][0])

    prepare(0)
    coming = dot(ready[0][1], f1_ref[:, steps[0][1]])
    for n, (i, cols) in enumerate(steps):
        x = coming
        if n + 3 < len(steps) and steps[n + 3][0] == len(ready):
            prepare(len(ready))
        if n + 1 < len(steps):
            later, ahead = steps[n + 1]
            coming = dot(ready[later][1], f1_ref[:, ahead])
        total[i] += dot(gelu(x).astype(BF), f2_ref[cols, :])
        if cols.stop == MLP:
            out_ref[block(i), :] = total[i].astype(BF)
            done(i)


def whole_kernel(
    feats_hbm,
    nbr_ref,
    rank_ref,
    cw_hbm,
    cpe_ref,
    n1_ref,
    wq_hbm,
    wk_hbm,
    wv_hbm,
    wp_hbm,
    n2_ref,
    f1_hbm,
    f2_hbm,
    out_hbm,
    ext,
    cw,
    wqkv,
    wp,
    f1,
    f2,
    yb,
    yf,
    conv_all,
    placed_all,
    merged_all,
    h1,
    normed,
    note_out,
    note_in,
    there_out,
    there_in,
    back_out,
    back_in,
    to_place,
    from_place,
    from_bucket,
    qq,
    keys,
    values,
    acc,
    att,
    result,
    load_sem,
    halo_send,
    halo_recv,
    block_send,
    block_recv,
    gather_send,
    gather_recv,
    store_sem,
):
    p = lax.axis_index("pts")
    h = lax.axis_index("head")
    loads = [
        pltpu.make_async_copy(source, target, load_sem.at[i])
        for i, (source, target) in enumerate(
            (
                (feats_hbm, ext.at[pl.ds(REACH, PTS)]),
                (cw_hbm, cw),
                (wq_hbm, wqkv.at[:, pl.ds(0, W)]),
                (wk_hbm, wqkv.at[:, pl.ds(W, W)]),
                (wv_hbm, wqkv.at[:, pl.ds(2 * W, W)]),
                (wp_hbm, wp),
                (f1_hbm, f1),
                (f2_hbm, f2),
            )
        )
    ]
    for load in loads:
        load.start()
    barrier_signal(p, h)
    bucket, positions = bucket_of(rank_ref[...])
    note_out[...] = note_rows(positions)
    loads[0].wait()
    loads[1].wait()
    inner = pl.ds(REACH, PTS)
    conv_project(ext, inner, inner, cw, 0, MID + 1, yb)
    barrier_wait()

    halos = [
        pltpu.make_async_remote_copy(
            src_ref=feats_hbm.at[pl.ds(first, REACH)],
            dst_ref=ext.at[pl.ds(to, REACH)],
            send_sem=halo_send.at[i],
            recv_sem=halo_recv.at[i],
            device_id=(lax.rem(p + step, DEVS), h),
            device_id_type=MESH,
        )
        for i, (first, to, step) in enumerate(
            ((PTS - REACH, 0, 1), (0, PTS + REACH, DEVS - 1))
        )
    ]
    for halo in halos:
        halo.start()
    conv_project(ext, inner, pl.ds(0, PTS), cw, MID + 1, MID, yf)

    gathers = [
        Gather(p, h, ref, gather_send.at[i], gather_recv.at[i])
        for i, ref in enumerate(
            [conv_all] + [ref.at[w] for ref in (placed_all, merged_all) for w in range(2)]
        )
    ]
    gather = gathers[0]

    def convolve(c):
        conv_all[h, block(c), :] = conv_select(c, p * PTS, nbr_ref, yb, yf).astype(BF)
        gather.start(c)

    def norm(c):
        gather.finish(c)
        mid_block(c, conv_all, ext, cpe_ref, n1_ref, h1, normed)

    @pl.loop(1, 3)
    def _(c):
        convolve(c)

    for halo in halos:
        halo.wait_recv()

    for k in range(1, DEVS):
        d = lax.rem(p + k, DEVS)
        send_block(p, h, d, NOTE, note_out, note_in, block_send.at[0], block_recv.at[0])

    note_in[block(p, NOTE), :] = note_out[block(p, NOTE), :]

    conv_project(ext, pl.ds(0, REACH), pl.ds(0, REACH), cw, 0, MID, yb)
    after = pl.ds(PTS + REACH, REACH)
    conv_project(ext, after, pl.ds(PTS, REACH), cw, MID + 1, MID, yf)

    @pl.loop(0, 2)
    def _(j):
        convolve(3 * j)
        norm(1 + j)


    @pl.loop(0, ROWS // BLK)
    def _(b):
        from_place[block(b), :] = hot(iota((BLK, PTS), 0) + b * BLK == bucket)

    norm(0)
    norm(3)

    x, z, core = p // GROUP, lax.rem(p, GROUP) // 2, lax.rem(p, 2)

    def send_wave(w, b, out_ref, in_ref, i):
        def send(d):
            send_block(
                p, h, d, HALF, out_ref.at[w], in_ref.at[w],
                block_send.at[i + w], block_recv.at[i + w],
            )

        for ahead in (4, 3, 5, 2, 6, 1, 7):
            chip = b * GROUP + 2 * lax.rem(z + ahead, GROUP // 2)
            send(chip)
            send(chip + 1)
        chip = b * GROUP + 2 * z
        send(chip + 1 - core)

        @pl.when(b != x)
        def _():
            send(chip + core)

    def turn_of(j):
        return lax.rem(x + 2 + 3 * j, CHUNKS)

    def keep_own(w, out_ref, in_ref):
        in_ref[w, block(p, HALF), :] = out_ref[w, block(p, HALF), :]

    own = normed[h]
    own = jnp.concatenate([own, turned(own)], 1)

    def both_halves(b, right):
        left = jnp.concatenate([from_place[block(b), :], from_place[block(b + CHUNKS), :]], 0)
        product = dot(left, right)
        return product[:BLK], product[BLK:]

    @pl.loop(0, CHUNKS)
    def _(j):
        b = turn_of(j)
        low, high = both_halves(b, own)
        there_out[0, block(b), :] = beside(low[:, :W], high[:, W:]).astype(BF)
        there_out[1, block(b), :] = beside(low[:, W:], high[:, :W]).astype(BF)
        send_wave(0, b, there_out, there_in, 1)

    for w in range(2):
        keep_own(w, there_out, there_in)
    wait_blocks(NOTE, note_in, block_recv.at[0])
    spots = spots_of(note_in[...])

    @pl.loop(0, CHUNKS)
    def _(c):
        to_place[block(c), :] = hot(iota((BLK, ROWS), 0) + c * BLK == spots)

    @pl.loop(0, CHUNKS)
    def _(j):
        send_wave(1, turn_of(j), there_out, there_in, 1)

    def unbundle(w, in_ref, i, chosen, all_ref, gather):
        wait_blocks(HALF, in_ref.at[w], block_recv.at[i + w])
        half = BLK // 2
        for c in range(CHUNKS):
            low = dot(chosen[block(c), :SIDE], in_ref[w])
            high = dot(chosen[block(c), SIDE:], in_ref[w])
            first = low[:half] + pltpu.roll(high[:half], WAVE, 1)
            last = pltpu.roll(low[half:], WAVE, 1) + high[half:]
            all_ref[w, h, block(c, half), :] = beside(first, last).astype(BF)
            gather.start(c)

    unbundle(0, there_in, 1, to_place, placed_all, gathers[1])
    spots_column = column_of(spots)
    for k in range(0, ROWS, BLK):
        from_place[k : k + BLK, :] = hot(iota((BLK, PTS), 1) == spots_column[k : k + BLK, :])
    unbundle(1, there_in, 1, to_place, placed_all, gathers[2])
    bucket_column = column_of(bucket)
    for k in range(0, PTS, BLK):
        from_bucket[k : k + BLK, :] = hot(iota((BLK, ROWS), 1) == bucket_column[k : k + BLK, :])
    for load in loads[2:5]:
        load.wait()

    @pl.loop(0, CHUNKS)
    def _(c):
        gathers[1].finish(c)
        gathers[2].finish(c)
        project_qkv(c, placed_all, wqkv, qq, keys, values)

    for w in range(2):
        attend(w, qq, keys, values, acc, att)

        @pl.loop(0, CHUNKS)
        def _(j):
            b = turn_of(j)
            low, high = both_halves(b, att[...])
            back_out[w, block(b), :] = beside(low[:, :W], high[:, W:]).astype(BF)
            send_wave(w, b, back_out, back_in, 3)

        keep_own(w, back_out, back_in)

    unbundle(0, back_in, 3, from_bucket, merged_all, gathers[3])
    unbundle(1, back_in, 3, from_bucket, merged_all, gathers[4])
    for load in loads[5:]:
        load.wait()

    def store(c):
        return pltpu.make_async_copy(
            result.at[block(c)], out_hbm.at[block(c)], store_sem.at[c]
        )

    def merged_there(c):
        gathers[3].finish(c)
        gathers[4].finish(c)

    mlp_blocks(
        merged_there, lambda c: store(c).start(),
        merged_all, h1, wp, n2_ref, f1, f2, result,
    )

    for halo in halos:
        halo.wait_send()
    wait_blocks(NOTE, note_out, block_send.at[0])
    for w in range(2):
        wait_blocks(HALF, there_out.at[w], block_send.at[1 + w])
        wait_blocks(HALF, back_out.at[w], block_send.at[3 + w])
    for gather in gathers:
        gather.drain()
    for c in range(CHUNKS):
        store(c).wait()


def per_device(
    feats,
    neighbours,
    rank,
    conv_weight,
    cpe_gain,
    norm1_gain,
    w_query,
    w_key,
    w_value,
    w_proj,
    norm2_gain,
    w_fc1,
    w_fc2,
):
    here, there = pl.BlockSpec(memory_space=VMEM), pl.BlockSpec(memory_space=pl.ANY)
    dma = pltpu.SemaphoreType.DMA
    return pl.pallas_call(
        whole_kernel,
        out_shape=jax.ShapeDtypeStruct((PTS, C), BF),
        in_specs=[there, here, here, there, here, here] + [there] * 4 + [here, there, there],
        out_specs=there,
        scratch_shapes=[
            pltpu.VMEM((PTS + 2 * REACH, C), BF),
            pltpu.VMEM((TAPS, C, W), BF),
            pltpu.VMEM((C, 3 * W), BF),
            pltpu.VMEM((C, C), BF),
            pltpu.VMEM((C, MLP), BF),
            pltpu.VMEM((MLP, C), BF),
            pltpu.VMEM((MID + 1, PTS + REACH, W), BF),
            pltpu.VMEM((MID, PTS + REACH, W), BF),
            pltpu.VMEM((HEADS, PTS, W), BF),
            pltpu.VMEM((2, HEADS, PTS // 2, W), BF),
            pltpu.VMEM((2, HEADS, PTS // 2, W), BF),
            pltpu.VMEM((PTS, C), F32),
            pltpu.VMEM((HEADS, PTS, W), BF),
            pltpu.VMEM((DEVS * NOTE, W), BF),
            pltpu.VMEM((DEVS * NOTE, W), BF),
            pltpu.VMEM((2, SIDE, W), BF),
            pltpu.VMEM((2, SIDE, W), BF),
            pltpu.VMEM((2, SIDE, W), BF),
            pltpu.VMEM((2, SIDE, W), BF),
            pltpu.VMEM((PTS, ROWS), BF),
            pltpu.VMEM((ROWS, PTS), BF),
            pltpu.VMEM((PTS, ROWS), BF),
            pltpu.VMEM((PTS, 2 * W), BF),
            pltpu.VMEM((PTS, W), BF),
            pltpu.VMEM((PTS, W), BF),
            pltpu.VMEM((PTS, 2 * W), F32),
            pltpu.VMEM((PTS, 2 * W), BF),
            pltpu.VMEM((PTS, C), BF),
            dma((8,)),
            dma((2,)),
            dma((2,)),
            dma((5,)),
            dma((5,)),
            dma((5, 3, CHUNKS)),
            dma((5, 3, CHUNKS)),
            dma((CHUNKS,)),
        ],
        compiler_params=pltpu.CompilerParams(
            collective_id=0, has_side_effects=True, vmem_limit_bytes=58 * 2**20
        ),
    )(
        feats,
        neighbours.T,
        rank.reshape(1, PTS),
        conv_weight,
        cpe_gain.reshape(1, C),
        norm1_gain.reshape(1, C),
        w_query,
        w_key,
        w_value,
        w_proj,
        norm2_gain.reshape(1, C),
        w_fc1,
        w_fc2,
    )


def solution(mesh):
    placed = (
        P("pts", None),
        P("pts", None),
        P("pts"),
        P(None, None, "head"),
        P(),
        P(),
        P(None, "head"),
        P(None, "head"),
        P(None, "head"),
        P(),
        P(),
        P(),
        P(),
    )
    return jax.shard_map(
        per_device, mesh=mesh, in_specs=placed, out_specs=P("pts", None), check_vma=False
    )
```

```python
import jax
import jax.numpy as jnp
import numpy as np
from jax import lax
from jax.experimental import pallas as pl
from jax.experimental.pallas import tpu as pltpu
from jax.sharding import PartitionSpec as P

HD = 16
PTS = 1024
REACH = 256
TAPS = 27
MID = 13
C = 512
MLP = 2048
W = 128
HEADS = 4
DEVS = 64
SLOTS = 32
HALF = SLOTS // 2
SIDE = DEVS * HALF
ROWS = DEVS * SLOTS
WAVE = 64
NOTE = 16
BLK = 256
CHUNKS = PTS // BLK
GROUP = BLK // HALF
BF = jnp.bfloat16
F32 = jnp.float32
I32 = jnp.int32
MESH = pl.DeviceIdType.MESH


def iota(shape, dim):
    return lax.broadcasted_iota(I32, shape, dim)


def dot(a, b):
    return jnp.dot(a, b, preferred_element_type=F32)


def dot_nt(a, b):
    return lax.dot_general(a, b, (((1,), (1,)), ((), ())), preferred_element_type=F32)


def hot(mask):
    return jnp.where(mask, 1.0, 0.0).astype(BF)


def turned(x):
    return pltpu.roll(x.astype(F32), WAVE, 1).astype(x.dtype)


def beside(low, high):
    return jnp.where(iota(low.shape, 1) < WAVE, low, high)


def block(a, size=BLK):
    return pl.ds(pl.multiple_of(a * size, size), size)


def barrier_signal(p, h):
    barrier = pltpu.get_barrier_semaphore()

    @pl.loop(1, DEVS)
    def _(k):
        pl.semaphore_signal(
            barrier, inc=1, device_id=(lax.rem(p + k, DEVS), h), device_id_type=MESH
        )

    for k in range(1, HEADS):
        pl.semaphore_signal(
            barrier, inc=1, device_id=(p, lax.rem(h + k, HEADS)), device_id_type=MESH
        )


def barrier_wait():
    pl.semaphore_wait(pltpu.get_barrier_semaphore(), DEVS - 1 + HEADS - 1)


def send_block(p, h, d, size, out_ref, in_ref, send_sem, recv_sem):
    pltpu.make_async_remote_copy(
        src_ref=out_ref.at[block(d, size)],
        dst_ref=in_ref.at[block(p, size)],
        send_sem=send_sem,
        recv_sem=recv_sem,
        device_id=(d, h),
        device_id_type=MESH,
    ).start()


def wait_blocks(size, ref, sem):
    part = ref.at[pl.ds(0, (DEVS - 1) * size)]
    pltpu.make_async_copy(part, part, sem).wait()


class Gather:
    def __init__(self, p, h, ref, send_sem, recv_sem):
        self.p, self.h, self.ref, self.send_sem, self.recv_sem = p, h, ref, send_sem, recv_sem
        self.size = ref.shape[1] // CHUNKS

    def copy(self, step, c, owner):
        rows = self.ref.at[owner, block(c, self.size)]
        return pltpu.make_async_remote_copy(
            src_ref=rows,
            dst_ref=rows,
            send_sem=self.send_sem.at[step - 1, c],
            recv_sem=self.recv_sem.at[step - 1, c],
            device_id=(self.p, lax.rem(self.h + step, HEADS)),
            device_id_type=MESH,
        )

    def start(self, c):
        for step in (2, 1, 3):
            self.copy(step, c, self.h).start()

    def finish(self, c):
        for step in (1, 3, 2):
            self.copy(step, c, lax.rem(self.h + HEADS - step, HEADS)).wait_recv()

    def drain(self):
        @pl.loop(0, CHUNKS)
        def _(c):
            for step in (1, 2, 3):
                self.copy(step, c, self.h).wait_send()


def conv_project(ext_ref, ext_rows, y_rows, w_ref, first, count, y_ref, y_first=0):
    for j in range(0, count, 2):
        if j + 1 < count:
            pair = jnp.concatenate([w_ref[first + j], w_ref[first + j + 1]], 1)
            y = dot(ext_ref[ext_rows, :], pair).astype(BF)
            y_ref[y_first + j, y_rows, :] = y[:, :W]
            y_ref[y_first + j + 1, y_rows, :] = y[:, W:]
        else:
            y = dot(ext_ref[ext_rows, :], w_ref[first + j])
            y_ref[y_first + j, y_rows, :] = y.astype(BF)


def conv_select(a, base, nbr_ref, yb_ref, yf_ref):
    start = pl.multiple_of(a * BLK, BLK)
    nbr = jnp.transpose(nbr_ref[:, pl.ds(start, BLK)])
    at = jnp.where(nbr < 0, -4096, nbr - (base + start))
    window = iota((BLK, 2 * BLK), 1)
    acc = yb_ref[MID, pl.ds(start + REACH, BLK), :].astype(F32)

    def select(t):
        place = at[:, t : t + 1] + (REACH if t < MID else 0)
        return hot(window == place)

    def rows(t):
        ref = yb_ref.at[t] if t < MID else yf_ref.at[t - MID - 1]
        return ref[pl.ds(start, 2 * BLK), :]

    taps = [t for t in range(TAPS) if t != MID]
    coming = select(taps[0])
    for t, later in zip(taps, taps[1:] + [None]):
        sel = coming
        if later is not None:
            coming = select(later)
        acc += dot(sel, rows(t))
    return acc


def norm_slices(parts, gain_ref):
    mean = sum(jnp.sum(p, 1, keepdims=True) for p in parts) * (1.0 / C)
    centre = [p - mean for p in parts]
    spread = sum(jnp.sum(c * c, 1, keepdims=True) for c in centre) * (1.0 / C)
    scale = lax.rsqrt(spread + 1e-05)
    return [c * scale * gain_ref[:, W * k : W * k + W] for k, c in enumerate(centre)]


def mid_block(a, conv_ref, ext_ref, cpe_ref, n1_ref, h1_ref, normed_ref):
    rows = block(a)
    feats = ext_ref[pl.ds(pl.multiple_of(a * BLK + REACH, BLK), BLK), :].astype(F32)
    normed = norm_slices([conv_ref[k, rows, :].astype(F32) for k in range(HEADS)], cpe_ref)
    h1 = [feats[:, W * k : W * k + W] + normed[k] for k in range(HEADS)]
    for k, part in enumerate(norm_slices(h1, n1_ref)):
        h1_ref[rows, W * k : W * k + W] = h1[k]
        normed_ref[k, rows, :] = part.astype(BF)


def column_of(row):
    same = iota((W, W), 0) == iota((W, W), 1)
    parts = [
        jnp.sum(jnp.where(same, row[:, k : k + W], 0), 1, keepdims=True)
        for k in range(0, row.shape[1], W)
    ]
    return jnp.concatenate(parts, 0)


def bucket_of(rank_row):
    target = rank_row // PTS
    member = iota((DEVS, PTS), 0) == target
    ones = jnp.where(member, 1.0, 0.0)
    upper = hot(iota((PTS, PTS), 0) < iota((PTS, PTS), 1))
    counts = dot(ones.astype(BF), upper)
    slot = jnp.sum(counts * ones, 0, keepdims=True).astype(I32)
    code = rank_row % PTS + 1
    by_slot = hot(iota((W, PTS), 0) == slot)
    high = dot_nt((ones * (code // 32).astype(F32)).astype(BF), by_slot)
    low = dot_nt((ones * (code % 32).astype(F32)).astype(BF), by_slot)
    row = slot // HALF * SIDE + target * HALF + slot % HALF
    return row, jnp.concatenate([high, low], 0).astype(BF)


def note_rows(positions):
    r = iota((DEVS * NOTE, W), 0)
    c = iota((DEVS * NOTE, W), 1)
    d = r // NOTE
    place = hot(((r % NOTE == 0) & (c == d)) | ((r % NOTE == 1) & (c == d + DEVS)))
    return dot(place, positions).astype(BF)


def spots_of(notes):
    r = iota((DEVS, DEVS * NOTE), 1)
    q = iota((DEVS, DEVS * NOTE), 0)
    high = dot(hot(r == q * NOTE), notes).astype(BF)
    low = dot(hot(r == q * NOTE + 1), notes).astype(BF)
    row = iota((W, ROWS), 1)
    pick = hot(iota((W, ROWS), 0) == row // SIDE * HALF + row % HALF)
    full = dot(high, pick) * 32.0 + dot(low, pick) - 1.0
    mine = iota((DEVS, ROWS), 0) == iota((DEVS, ROWS), 1) % SIDE // HALF
    return jnp.sum(jnp.where(mine, full, 0.0), 0, keepdims=True).astype(I32)


def joined(c, ref):
    rows = block(c, BLK // 2)
    parts = []
    for k in range(HEADS):
        first, last = ref[0, k, rows, :], ref[1, k, rows, :]
        parts.append(
            jnp.concatenate([beside(first, turned(last)), beside(turned(first), last)], 0)
        )
    return jnp.concatenate(parts, 1)


def project_qkv(c, x_ref, w_ref, qq_ref, k_ref, v_ref):
    rows = block(c)
    qkv = dot(joined(c, x_ref), w_ref[...]).astype(BF)
    scaled = qkv[:, :W].astype(F32) * np.float32(np.log2(np.e) / 4.0)
    high = scaled.astype(BF)
    qq_ref[rows, :W] = high
    qq_ref[rows, W:] = (scaled - high.astype(F32)).astype(BF)
    k_ref[rows, :] = qkv[:, W : 2 * W]
    v_ref[rows, :] = qkv[:, 2 * W :]


def attend(wave, qq_ref, k_ref, v_ref, acc_ref, att_ref):
    acc_ref[...] = jnp.zeros_like(acc_ref)
    lane = iota((PTS, W), 1) // HD
    heads = WAVE // HD

    def operands(head):
        own = lane == head
        zero = jnp.zeros((PTS, W), BF)
        keys = jnp.where(own, k_ref[...], zero)
        values = jnp.where(own, v_ref[...], zero)
        return jnp.concatenate([keys, keys], 1), jnp.concatenate([values, hot(own)], 1)

    def weigh(values, rows, probs):
        acc_ref[rows, :] += dot(probs, values)

    given = [operands(wave * heads + k) for k in range(heads)]
    steps = [(pair, slice(b, b + BLK)) for pair in given for b in range(0, PTS, BLK)]
    coming = dot_nt(qq_ref[steps[0][1], :], steps[0][0][0])
    behind = None
    for i, ((_, values), rows) in enumerate(steps):
        scores = coming
        if i + 1 < len(steps):
            (keys, _), later = steps[i + 1]
            coming = dot_nt(qq_ref[later, :], keys)
        if behind is not None:
            weigh(*behind)
        top = jnp.max(scores, 1, keepdims=True)
        behind = values, rows, jnp.exp2(scores - top).astype(BF)
    weigh(*behind)

    done = lane // heads == wave
    straight = jnp.where(done, acc_ref[:, :W] / jnp.where(done, acc_ref[:, W:], 1.0), 0.0)
    other = pltpu.roll(straight, WAVE, 1)
    first, last = (other, straight) if wave else (straight, other)
    att_ref[:, :W] = first.astype(BF)
    att_ref[:, W:] = last.astype(BF)


def gelu(x):
    return 0.5 * x * (1.0 + lax.erf(x * np.float32(np.sqrt(0.5))))


def mlp_rows(a, att_ref, h1_ref, wp_ref, n2_ref):
    merged = dot(joined(a, att_ref), wp_ref[...])
    h2 = h1_ref[block(a), :] + merged.astype(BF).astype(F32)
    parts = norm_slices([h2[:, W * k : W * k + W] for k in range(HEADS)], n2_ref)
    return h2, jnp.concatenate([part.astype(BF) for part in parts], 1)


def mlp_blocks(finish, done, att_ref, h1_ref, wp_ref, n2_ref, f1_ref, f2_ref, out_ref):
    width = C // 2
    steps = [(i, slice(j, j + width)) for i in range(CHUNKS) for j in range(0, MLP, width)]
    ready, total = [], []

    def prepare(c):
        finish(c)
        ready.append(mlp_rows(c, att_ref, h1_ref, wp_ref, n2_ref))
        total.append(ready[-1][0])

    def add(i, cols, hidden):
        total[i] += dot(hidden, f2_ref[cols, :])
        if cols.stop == MLP:
            out_ref[block(i), :] = total[i].astype(BF)
            done(i)

    prepare(0)
    coming = dot(ready[0][1], f1_ref[:, steps[0][1]])
    behind = None
    for n, (i, cols) in enumerate(steps):
        x = coming
        if n + 3 < len(steps) and steps[n + 3][0] == len(ready):
            prepare(len(ready))
        if n + 1 < len(steps):
            later, ahead = steps[n + 1]
            coming = dot(ready[later][1], f1_ref[:, ahead])
        if behind is not None:
            add(*behind)
        behind = i, cols, gelu(x).astype(BF)
    add(*behind)


def whole_kernel(
    feats_hbm,
    nbr_hbm,
    rank_hbm,
    cw_hbm,
    cpe_hbm,
    n1_hbm,
    wq_hbm,
    wk_hbm,
    wv_hbm,
    wp_hbm,
    n2_hbm,
    f1_hbm,
    f2_hbm,
    out_hbm,
    nbr_ref,
    rank_ref,
    cpe_ref,
    n1_ref,
    n2_ref,
    ext,
    cw,
    wqkv,
    wp,
    f1,
    f2,
    yb,
    yf,
    conv_all,
    placed_all,
    merged_all,
    h1,
    normed,
    note_out,
    note_in,
    there_out,
    there_in,
    back_out,
    back_in,
    to_place,
    from_place,
    from_bucket,
    qq,
    keys,
    values,
    acc,
    att,
    result,
    load_sem,
    halo_send,
    halo_recv,
    block_send,
    block_recv,
    gather_send,
    gather_recv,
    store_sem,
):
    p = lax.axis_index("pts")
    h = lax.axis_index("head")
    taps = ((0, 4), (4, MID + 1), (MID + 1, TAPS))
    loads = [
        pltpu.make_async_copy(source, target, load_sem.at[i])
        for i, (source, target) in enumerate(
            [(feats_hbm, ext.at[pl.ds(REACH, PTS)])]
            + [(cw_hbm.at[pl.ds(a, b - a)], cw.at[pl.ds(a, b - a)]) for a, b in taps]
            + [
                (rank_hbm, rank_ref),
                (nbr_hbm, nbr_ref),
                (cpe_hbm, cpe_ref),
                (n1_hbm, n1_ref),
                (wq_hbm, wqkv.at[:, pl.ds(0, W)]),
                (wk_hbm, wqkv.at[:, pl.ds(W, W)]),
                (wv_hbm, wqkv.at[:, pl.ds(2 * W, W)]),
                (wp_hbm, wp),
                (n2_hbm, n2_ref),
                (f1_hbm, f1),
                (f2_hbm, f2),
            ]
        )
    ]
    for load in loads:
        load.start()
    barrier_signal(p, h)
    inner = pl.ds(REACH, PTS)
    loads[0].wait()
    for (a, b), load in zip(taps[:2], loads[1:3]):
        load.wait()
        conv_project(ext, inner, inner, cw, a, b - a, yb, a)
    loads[4].wait()
    bucket, positions = bucket_of(rank_ref[...])
    note_out[...] = note_rows(positions)
    barrier_wait()

    halos = [
        pltpu.make_async_remote_copy(
            src_ref=feats_hbm.at[pl.ds(first, REACH)],
            dst_ref=ext.at[pl.ds(to, REACH)],
            send_sem=halo_send.at[i],
            recv_sem=halo_recv.at[i],
            device_id=(lax.rem(p + step, DEVS), h),
            device_id_type=MESH,
        )
        for i, (first, to, step) in enumerate(
            ((PTS - REACH, 0, 1), (0, PTS + REACH, DEVS - 1))
        )
    ]
    for halo in halos:
        halo.start()
    loads[3].wait()
    conv_project(ext, inner, pl.ds(0, PTS), cw, MID + 1, MID, yf)

    gathers = [
        Gather(p, h, ref, gather_send.at[i], gather_recv.at[i])
        for i, ref in enumerate(
            [conv_all] + [ref.at[w] for ref in (placed_all, merged_all) for w in range(2)]
        )
    ]
    gather = gathers[0]

    def convolve(c):
        conv_all[h, block(c), :] = conv_select(c, p * PTS, nbr_ref, yb, yf).astype(BF)
        gather.start(c)

    def norm(c):
        gather.finish(c)
        mid_block(c, conv_all, ext, cpe_ref, n1_ref, h1, normed)

    for load in loads[5:8]:
        load.wait()

    @pl.loop(1, 3)
    def _(c):
        convolve(c)

    for halo in halos:
        halo.wait_recv()

    for k in range(1, DEVS):
        d = lax.rem(p + k, DEVS)
        send_block(p, h, d, NOTE, note_out, note_in, block_send.at[0], block_recv.at[0])

    note_in[block(p, NOTE), :] = note_out[block(p, NOTE), :]

    conv_project(ext, pl.ds(0, REACH), pl.ds(0, REACH), cw, 0, MID, yb)
    after = pl.ds(PTS + REACH, REACH)
    conv_project(ext, after, pl.ds(PTS, REACH), cw, MID + 1, MID, yf)

    @pl.loop(0, 2)
    def _(j):
        convolve(3 * j)

    @pl.loop(1, 3)
    def _(c):
        norm(c)


    @pl.loop(0, ROWS // BLK)
    def _(b):
        from_place[block(b), :] = hot(iota((BLK, PTS), 0) + b * BLK == bucket)

    norm(0)
    norm(3)

    x, z, core = p // GROUP, lax.rem(p, GROUP) // 2, lax.rem(p, 2)

    def send_wave(w, b, out_ref, in_ref, i):
        def send(d):
            send_block(
                p, h, d, HALF, out_ref.at[w], in_ref.at[w],
                block_send.at[i + w], block_recv.at[i + w],
            )

        for ahead in (4, 3, 5, 2, 6, 1, 7):
            chip = b * GROUP + 2 * lax.rem(z + ahead, GROUP // 2)
            send(chip)
            send(chip + 1)
        chip = b * GROUP + 2 * z
        send(chip + 1 - core)

        @pl.when(b != x)
        def _():
            send(chip + core)

    def turn_of(j):
        return lax.rem(x + 2 + 3 * j, CHUNKS)

    def keep_own(w, out_ref, in_ref):
        in_ref[w, block(p, HALF), :] = out_ref[w, block(p, HALF), :]

    own = normed[h]
    own = jnp.concatenate([own, turned(own)], 1)

    def both_halves(b, right):
        left = jnp.concatenate([from_place[block(b), :], from_place[block(b + CHUNKS), :]], 0)
        product = dot(left, right)
        return product[:BLK], product[BLK:]

    @pl.loop(0, CHUNKS)
    def _(j):
        b = turn_of(j)
        low, high = both_halves(b, own)
        there_out[0, block(b), :] = beside(low[:, :W], high[:, W:]).astype(BF)
        there_out[1, block(b), :] = beside(low[:, W:], high[:, :W]).astype(BF)
        send_wave(0, b, there_out, there_in, 1)

    for w in range(2):
        keep_own(w, there_out, there_in)
    wait_blocks(NOTE, note_in, block_recv.at[0])
    spots = spots_of(note_in[...])

    @pl.loop(0, CHUNKS)
    def _(c):
        to_place[block(c), :] = hot(iota((BLK, ROWS), 0) + c * BLK == spots)

    spots_column = column_of(spots)
    for k in range(0, ROWS, BLK):
        from_place[k : k + BLK, :] = hot(iota((BLK, PTS), 1) == spots_column[k : k + BLK, :])

    @pl.loop(0, CHUNKS)
    def _(j):
        send_wave(1, turn_of(j), there_out, there_in, 1)

    def unbundle(w, in_ref, i, chosen, all_ref, gather):
        wait_blocks(HALF, in_ref.at[w], block_recv.at[i + w])
        half = BLK // 2
        for c in range(CHUNKS):
            low = dot(chosen[block(c), :SIDE], in_ref[w])
            high = dot(chosen[block(c), SIDE:], in_ref[w])
            first = low[:half] + pltpu.roll(high[:half], WAVE, 1)
            last = pltpu.roll(low[half:], WAVE, 1) + high[half:]
            all_ref[w, h, block(c, half), :] = beside(first, last).astype(BF)
            gather.start(c)

    unbundle(0, there_in, 1, to_place, placed_all, gathers[1])
    unbundle(1, there_in, 1, to_place, placed_all, gathers[2])
    bucket_column = column_of(bucket)
    for k in range(0, PTS, BLK):
        from_bucket[k : k + BLK, :] = hot(iota((BLK, ROWS), 1) == bucket_column[k : k + BLK, :])
    for load in loads[8:11]:
        load.wait()

    @pl.loop(0, CHUNKS)
    def _(c):
        gathers[1].finish(c)
        gathers[2].finish(c)
        project_qkv(c, placed_all, wqkv, qq, keys, values)

    for w in range(2):
        attend(w, qq, keys, values, acc, att)

        @pl.loop(0, CHUNKS)
        def _(j):
            b = turn_of(j)
            low, high = both_halves(b, att[...])
            back_out[w, block(b), :] = beside(low[:, :W], high[:, W:]).astype(BF)
            send_wave(w, b, back_out, back_in, 3)

        keep_own(w, back_out, back_in)

    unbundle(0, back_in, 3, from_bucket, merged_all, gathers[3])
    unbundle(1, back_in, 3, from_bucket, merged_all, gathers[4])
    for load in loads[11:]:
        load.wait()

    def store(c):
        return pltpu.make_async_copy(
            result.at[block(c)], out_hbm.at[block(c)], store_sem.at[c]
        )

    def merged_there(c):
        gathers[3].finish(c)
        gathers[4].finish(c)

    mlp_blocks(
        merged_there, lambda c: store(c).start(),
        merged_all, h1, wp, n2_ref, f1, f2, result,
    )

    for halo in halos:
        halo.wait_send()
    wait_blocks(NOTE, note_out, block_send.at[0])
    for w in range(2):
        wait_blocks(HALF, there_out.at[w], block_send.at[1 + w])
        wait_blocks(HALF, back_out.at[w], block_send.at[3 + w])
    for gather in gathers:
        gather.drain()
    for c in range(CHUNKS):
        store(c).wait()


def per_device(
    feats,
    neighbours,
    rank,
    conv_weight,
    cpe_gain,
    norm1_gain,
    w_query,
    w_key,
    w_value,
    w_proj,
    norm2_gain,
    w_fc1,
    w_fc2,
):
    there = pl.BlockSpec(memory_space=pl.ANY)
    dma = pltpu.SemaphoreType.DMA
    return pl.pallas_call(
        whole_kernel,
        out_shape=jax.ShapeDtypeStruct((PTS, C), BF),
        in_specs=[there] * 13,
        out_specs=there,
        scratch_shapes=[
            pltpu.VMEM((TAPS, PTS), I32),
            pltpu.VMEM((1, PTS), I32),
            pltpu.VMEM((1, C), F32),
            pltpu.VMEM((1, C), F32),
            pltpu.VMEM((1, C), F32),
            pltpu.VMEM((PTS + 2 * REACH, C), BF),
            pltpu.VMEM((TAPS, C, W), BF),
            pltpu.VMEM((C, 3 * W), BF),
            pltpu.VMEM((C, C), BF),
            pltpu.VMEM((C, MLP), BF),
            pltpu.VMEM((MLP, C), BF),
            pltpu.VMEM((MID + 1, PTS + REACH, W), BF),
            pltpu.VMEM((MID, PTS + REACH, W), BF),
            pltpu.VMEM((HEADS, PTS, W), BF),
            pltpu.VMEM((2, HEADS, PTS // 2, W), BF),
            pltpu.VMEM((2, HEADS, PTS // 2, W), BF),
            pltpu.VMEM((PTS, C), F32),
            pltpu.VMEM((HEADS, PTS, W), BF),
            pltpu.VMEM((DEVS * NOTE, W), BF),
            pltpu.VMEM((DEVS * NOTE, W), BF),
            pltpu.VMEM((2, SIDE, W), BF),
            pltpu.VMEM((2, SIDE, W), BF),
            pltpu.VMEM((2, SIDE, W), BF),
            pltpu.VMEM((2, SIDE, W), BF),
            pltpu.VMEM((PTS, ROWS), BF),
            pltpu.VMEM((ROWS, PTS), BF),
            pltpu.VMEM((PTS, ROWS), BF),
            pltpu.VMEM((PTS, 2 * W), BF),
            pltpu.VMEM((PTS, W), BF),
            pltpu.VMEM((PTS, W), BF),
            pltpu.VMEM((PTS, 2 * W), F32),
            pltpu.VMEM((PTS, 2 * W), BF),
            pltpu.VMEM((PTS, C), BF),
            dma((15,)),
            dma((2,)),
            dma((2,)),
            dma((5,)),
            dma((5,)),
            dma((5, 3, CHUNKS)),
            dma((5, 3, CHUNKS)),
            dma((CHUNKS,)),
        ],
        compiler_params=pltpu.CompilerParams(
            collective_id=0, has_side_effects=True, vmem_limit_bytes=58 * 2**20
        ),
    )(
        feats,
        neighbours.T,
        rank.reshape(1, PTS),
        conv_weight,
        cpe_gain.reshape(1, C),
        norm1_gain.reshape(1, C),
        w_query,
        w_key,
        w_value,
        w_proj,
        norm2_gain.reshape(1, C),
        w_fc1,
        w_fc2,
    )


def solution(mesh):
    placed = (
        P("pts", None),
        P("pts", None),
        P("pts"),
        P(None, None, "head"),
        P(),
        P(),
        P(None, "head"),
        P(None, "head"),
        P(None, "head"),
        P(),
        P(),
        P(),
        P(),
    )
    return jax.shard_map(
        per_device, mesh=mesh, in_specs=placed, out_specs=P("pts", None), check_vma=False
    )
```
